1024 devices in a mesh: gx: 16 (over x, z_lo), gy: 8 (over y), gz: 8 (over z_hi, core).
Axes of the slice: x: 4, y: 8, z: 16 (z_hi: 4, z_lo: 4; z = z_hi * 4 + z_lo), core: 2. Of those that a mesh axis runs over, the one named last changes fastest.
Arguments:
- tokens: bfloat16 [384, 6144], P(('gx', 'gy'), 'gz'), may hold values from -6 to 6
- w_up: bfloat16 [6144, 49152], P('gz', ('gx', 'gy')), may hold values from -0.078125 to 0.078125
- w_down: bfloat16 [49152, 6144], P(('gx', 'gy'), 'gz'), may hold values from -0.02734375 to 0.02734375
- cotangent: bfloat16 [384, 6144], P(('gx', 'gy'), 'gz'), may hold values from -6 to 6
Outputs:
- grad_in: float32 [384, 6144], P(('gx', 'gy'), 'gz')
- grad_up: bfloat16 [6144, 49152], P('gz', ('gx', 'gy'))
- grad_down: bfloat16 [49152, 6144], P(('gx', 'gy'), 'gz')
The draws below stay inside these ranges and needn't reach their ends.
All inputs are finite; a program needn't handle non-finite values.
Results may differ from the reference program's by a relative error of at most 0.0049.
Values may be sent and summed in bfloat16 or wider, within the bound.
A program may use at most 32 MiB of HBM per device.

```python
import math
import jax
import jax.numpy as jnp

D = 6144
FF = 49152
TOKENS = 384


def level_of(rng, shape, split, least, high):
    factor_of, own = 1.0, jax.random.fold_in(rng, 6)
    for axis_at, blocks in split:
        steps = jnp.exp(jax.random.uniform(jax.random.fold_in(own, axis_at), (blocks,), jnp.float32, least / len(split), high / len(split)))
        factor_of = factor_of * jnp.repeat(steps, shape[axis_at] // blocks).reshape([-1 if axis == axis_at else 1 for axis in range(len(shape))])
    return factor_of


def noise(key, extent, spread, bound, cuts=(), dtype=jnp.bfloat16):
    array = spread * jax.random.normal(key, extent, jnp.float32)
    if cuts:
        array = array * level_of(key, extent, cuts, -0.22, 0.18)
    return jnp.clip(array, -bound, bound).astype(dtype)


def setup_inputs(seed: int = 0) -> dict:
    key_of = jax.random.split(jax.random.key(seed), 5)
    return {
        "tokens": noise(key_of[0], (TOKENS, D), 1.0, 6.0, ((0, 128), (1, 8))),
        "w_up": noise(key_of[1], (D, FF), D ** -0.5, 0.078125, ((0, 8), (1, 128))),
        "w_down": noise(key_of[2], (FF, D), FF ** -0.5, 0.02734375, ((0, 128), (1, 8))),
        "cotangent": noise(key_of[3], (TOKENS, D), 1.0, 6.0, ((0, 128), (1, 8))),
    }


GELU_SCALE = math.sqrt(2.0 / math.pi)
CUBIC_COEFF = 0.044715

def activate(pre_act, back_grad):
    squared = pre_act * pre_act
    tangent = jnp.tanh(GELU_SCALE * pre_act * (1.0 + CUBIC_COEFF * squared))
    hidden = (0.5 * pre_act * (1.0 + tangent)).astype(jnp.bfloat16)
    gelu_slope = 0.5 * (1.0 + tangent) + 0.5 * pre_act * (1.0 - tangent * tangent) * GELU_SCALE * (1.0 + 3.0 * CUBIC_COEFF * squared)
    return (hidden, (back_grad * gelu_slope).astype(jnp.bfloat16))

def reference(tokens, w_up, w_down, cotangent):
    pre_act = jnp.dot(tokens, w_up, preferred_element_type=jnp.float32)
    back_grad = jnp.dot(cotangent, w_down.T, preferred_element_type=jnp.float32)
    hidden, pre_grad = activate(pre_act, back_grad)
    grad_up = jnp.dot(tokens.T, pre_grad, preferred_element_type=jnp.float32).astype(jnp.bfloat16)
    grad_down = jnp.dot(hidden.T, cotangent, preferred_element_type=jnp.float32).astype(jnp.bfloat16)
    grad_in = jnp.dot(pre_grad, w_up.T, preferred_element_type=jnp.float32)
    return (grad_in, grad_up, grad_down)
```

```python
import functools
import math

import jax
import jax.numpy as jnp
from jax import lax
from jax.experimental import pallas as pl
from jax.experimental.pallas import tpu as pltpu
from jax.sharding import PartitionSpec as P

GELU_SCALE = math.sqrt(2.0 / math.pi)
CUBIC_COEFF = 0.044715
MESH = pl.DeviceIdType.MESH
BF16, F32 = jnp.bfloat16, jnp.float32
CHUNKS = 3


def activate(pre_act, back_grad):
    squared = pre_act * pre_act
    tangent = jnp.tanh(GELU_SCALE * pre_act * (1.0 + CUBIC_COEFF * squared))
    hidden = (0.5 * pre_act * (1.0 + tangent)).astype(BF16)
    gelu_slope = 0.5 * (1.0 + tangent) + 0.5 * pre_act * (1.0 - tangent * tangent) * GELU_SCALE * (
        1.0 + 3.0 * CUBIC_COEFF * squared
    )
    return hidden, (back_grad * gelu_slope).astype(BF16)


def slot_of(offset):
    return 0 if offset == 0 else 2 * offset - 1 if offset > 0 else -2 * offset


def dot_nt(a, b):
    return lax.dot_general(a, b, (((1,), (1,)), ((), ())), preferred_element_type=F32)


def dot_tn(a, b):
    return lax.dot_general(a, b, (((0,), (0,)), ((), ())), preferred_element_type=F32)


def kernel(
    sizes,
    tokens_ref, w_up_ref, w_down_ref, cot_ref,
    grad_in_ref, grad_up_ref, grad_down_ref,
    near, rows, wide, up, down, part, other, z1_out, z1_in, z2_out, z2_in, act,
    back, back_in, own48, last_out, last_in,
    local_sem, near_send, near_recv, y_send, y_recv, core_send, core_recv,
    z_send, z_recv, act_send, act_recv, back_send, back_recv, last_send, last_recv,
):
    n_gx, n_gy, n_gz = sizes
    n_hi = n_gz // 2
    own_rows = tokens_ref.shape[0]
    slot_rows = n_gx * own_rows
    total_rows = n_gy * slot_rows
    chunk_rows = total_rows // CHUNKS
    gx, gy, gz = lax.axis_index("gx"), lax.axis_index("gy"), lax.axis_index("gz")
    hi, core = gz // 2, gz % 2

    def at_gx(j):
        return ((gx + j) % n_gx, gy, gz)

    def at_gy(j):
        return (gx, (gy + n_gy + j) % n_gy, gz)

    def at_hi(j):
        return (gx, gy, ((hi + n_hi + j) % n_hi) * 2 + core)

    other_core = (gx, gy, hi * 2 + 1 - core)

    load_up = pltpu.make_async_copy(w_up_ref, up, local_sem.at[0])
    load_down = pltpu.make_async_copy(w_down_ref, down, local_sem.at[1])
    load_tokens = pltpu.make_async_copy(tokens_ref, near.at[gx, 0], local_sem.at[2])
    load_cot = pltpu.make_async_copy(cot_ref, near.at[gx, 1], local_sem.at[3])
    load_tokens.start()
    load_cot.start()
    load_up.start()
    load_down.start()

    partners = [at_gx(j) for j in range(1, n_gx)] + [at_gy(j) for j in range(1, n_gy)]
    partners += [at_hi(1), at_hi(-1), other_core]
    barrier = pltpu.get_barrier_semaphore()
    for partner in partners:
        pl.semaphore_signal(barrier, inc=1, device_id=partner, device_id_type=MESH)
    load_tokens.wait()
    load_cot.wait()
    pl.semaphore_wait(barrier, len(partners))

    sent = []

    def send(src, dst, send_sem, recv_sem, device):
        copy = pltpu.make_async_remote_copy(
            src_ref=src, dst_ref=dst, send_sem=send_sem, recv_sem=recv_sem, device_id=device, device_id_type=MESH
        )
        copy.start()
        sent.append(copy)

    def arrived(dst, recv_sem):
        pltpu.make_async_remote_copy(
            src_ref=dst, dst_ref=dst, send_sem=recv_sem, recv_sem=recv_sem, device_id=other_core, device_id_type=MESH
        ).wait_recv()

    for j in range(1, n_gx):
        send(near.at[gx], near.at[gx], near_send.at[j], near_recv.at[j], at_gx(j))
    for j in range(1, n_gx):
        arrived(near.at[(gx + n_gx - j) % n_gx], near_recv.at[j])
    for u in range(n_gx):
        for which in range(2):
            wide[which, u * own_rows : (u + 1) * own_rows] = near[u, which].astype(F32)
    rows[:, :slot_rows] = wide[...].astype(BF16)

    half = n_gy // 2
    split = slot_rows // 3 // 16 * 16

    def slot(offset, start=0, stop=slot_rows):
        first = slot_of(offset) * slot_rows
        return rows.at[:, first + start : first + stop]

    def ring(step):
        if step < half:
            send(slot(step - 1), slot(step), y_send.at[0, step], y_recv.at[0, step], at_gy(-1))
            send(slot(1 - step), slot(-step), y_send.at[1, step], y_recv.at[1, step], at_gy(1))
        else:
            lower, upper = (0, split), (split, slot_rows)
            send(slot(half - 1, *upper), slot(half, *upper), y_send.at[0, step], y_recv.at[0, step], at_gy(-1))
            send(slot(1 - half, *lower), slot(half, *lower), y_send.at[1, step], y_recv.at[1, step], at_gy(1))

    def ring_arrived(step):
        if step < half:
            arrived(slot(step), y_recv.at[0, step])
            arrived(slot(-step), y_recv.at[1, step])
        else:
            arrived(slot(half, split, slot_rows), y_recv.at[0, step])
            arrived(slot(half, 0, split), y_recv.at[1, step])

    right, left, across = (hi + 1) % n_hi, (hi + n_hi - 1) % n_hi, (hi + 2) % n_hi

    def chunk(c):
        return pl.ds(c * chunk_rows, chunk_rows)

    def forward(c):
        for which, value in enumerate(
            (
                jnp.dot(rows[0, chunk(c)], up[...], preferred_element_type=F32),
                dot_nt(rows[1, chunk(c)], down[...]),
            )
        ):
            part[c, :, which] = value.reshape(n_gz, chunk_rows // n_gz, value.shape[1])
        theirs = part.at[c, pl.ds((1 - core) * n_hi, n_hi)]
        send(theirs, other.at[c], core_send.at[c, 0], core_recv.at[c, 0], other_core)

    def mine(c, h, which):
        return part[c, core * n_hi + h, which] + other[c, h, which]

    def z1(c):
        arrived(other.at[c], core_recv.at[c, 0])
        for which, to in ((0, 1), (1, -1)):
            z1_out[c, which] = mine(c, across, which).astype(BF16)
            send(z1_out.at[c, which], z1_in.at[c, which], z_send.at[c, which], z_recv.at[c, which], at_hi(to))

    def z2(c):
        arrived(z1_in.at[c, 0], z_recv.at[c, 0])
        z2_out[c, 0, 0] = (mine(c, right, 0) + z1_in[c, 0].astype(F32)).astype(BF16)
        z2_out[c, 0, 1] = mine(c, right, 1).astype(BF16)
        send(z2_out.at[c, 0], z2_in.at[c, 0], z_send.at[c, 2], z_recv.at[c, 2], at_hi(1))
        arrived(z1_in.at[c, 1], z_recv.at[c, 1])
        z2_out[c, 1, 0] = mine(c, left, 0).astype(BF16)
        z2_out[c, 1, 1] = (mine(c, left, 1) + z1_in[c, 1].astype(F32)).astype(BF16)
        send(z2_out.at[c, 1], z2_in.at[c, 1], z_send.at[c, 3], z_recv.at[c, 3], at_hi(-1))

    def held(c, h, k=core):
        return act.at[c, k * n_hi + h]

    def to_core(c, h, at):
        send(held(c, h), held(c, h), core_send.at[c, at], core_recv.at[c, at], other_core)

    def z3(c):
        arrived(z2_in.at[c, 0], z_recv.at[c, 2])
        arrived(z2_in.at[c, 1], z_recv.at[c, 3])
        pre_act, back_grad = (
            mine(c, hi, which) + z2_in[c, 0, which].astype(F32) + z2_in[c, 1, which].astype(F32) for which in range(2)
        )
        hidden, pre_grad = activate(pre_act, back_grad)
        act[c, gz % 2 * n_hi + hi, 0] = hidden
        act[c, gz % 2 * n_hi + hi, 1] = pre_grad
        send(held(c, hi), held(c, hi), act_send.at[c, 0], act_recv.at[c, 0], at_hi(1))
        send(held(c, hi), held(c, hi), act_send.at[c, 1], act_recv.at[c, 1], at_hi(-1))
        to_core(c, hi, 1)

    def z4(c):
        arrived(held(c, left), act_recv.at[c, 0])
        send(held(c, left).at[0], held(c, left).at[0], act_send.at[c, 2], act_recv.at[c, 2], at_hi(1))
        arrived(held(c, right), act_recv.at[c, 1])
        send(held(c, right).at[1], held(c, right).at[1], act_send.at[c, 3], act_recv.at[c, 3], at_hi(-1))
        to_core(c, left, 2)
        to_core(c, right, 3)

    def z5(c):
        arrived(held(c, across).at[0], act_recv.at[c, 2])
        arrived(held(c, across).at[1], act_recv.at[c, 3])
        to_core(c, across, 4)
        for at, h in ((1, hi), (2, left), (3, right), (4, across)):
            arrived(held(c, h, 1 - core), core_recv.at[c, at])

    def whole(c, which):
        return act[c, :, which].reshape(chunk_rows, act.shape[-1])

    tile = 16
    done = []

    def backward(c):
        value = dot_nt(whole(c, 1), up[...])
        first = c * chunk_rows
        back[first : first + chunk_rows] = value.astype(BF16)
        if c == 0:
            own48[...] = value[:slot_rows]
        for offset in range(1 - half, half + 1):
            at = slot_of(offset)
            if at and at not in done and (at + 1) * slot_rows <= first + chunk_rows:
                done.append(at)
                send(
                    back.at[at * slot_rows : (at + 1) * slot_rows], back_in.at[at],
                    back_send.at[at], back_recv.at[at], at_gy(offset),
                )

    ring(1)
    load_up.wait()
    load_down.wait()
    ring_arrived(1)
    ring(2)
    forward(0)
    ring_arrived(2)
    ring(3)
    z1(0)
    ring_arrived(3)
    ring(4)
    forward(1)
    z2(0)
    z1(1)
    ring_arrived(4)
    forward(2)
    z3(0)
    z2(1)
    z1(2)
    z4(0)
    z3(1)
    z2(2)
    z5(0)
    backward(0)
    z4(1)
    z3(2)
    z5(1)
    backward(1)
    z4(2)
    z5(2)
    backward(2)

    hidden = jnp.concatenate([whole(c, 0) for c in range(CHUNKS)])
    pre_grad = jnp.concatenate([whole(c, 1) for c in range(CHUNKS)])
    grad_up_ref[...] = dot_tn(rows[0], pre_grad).astype(BF16)
    grad_down_ref[...] = dot_tn(hidden, rows[1]).astype(BF16)

    for at in range(1, n_gy):
        arrived(back_in.at[at], back_recv.at[at])
        own48[...] += back_in[at].astype(F32)
    for u in range(n_gx):
        last_out[u] = own48[u * own_rows : (u + 1) * own_rows].astype(BF16)
    for j in range(1, n_gx):
        send(last_out.at[(gx + j) % n_gx], last_in.at[j], last_send.at[j], last_recv.at[j], at_gx(j))
    result = last_out[gx].astype(F32)
    for j in range(1, n_gx):
        arrived(last_in.at[j], last_recv.at[j])
        result += last_in[j].astype(F32)
    grad_in_ref[...] = result
    for copy in sent:
        copy.wait_send()


def on_device(sizes, tokens, w_up, w_down, cotangent):
    n_gx, n_gy, n_gz = sizes
    own_rows, width = tokens.shape
    units = w_up.shape[1]
    slot_rows = n_gx * own_rows
    total = slot_rows * n_gy
    n_hi = n_gz // 2
    r = total // CHUNKS // n_gz
    dma = pltpu.SemaphoreType.DMA
    return pl.pallas_call(
        functools.partial(kernel, sizes),
        out_shape=(
            jax.ShapeDtypeStruct((own_rows, width), F32),
            jax.ShapeDtypeStruct((width, units), BF16),
            jax.ShapeDtypeStruct((units, width), BF16),
        ),
        in_specs=[pl.BlockSpec(memory_space=pl.ANY)] * 4,
        out_specs=(pl.BlockSpec(memory_space=pltpu.VMEM),) * 3,
        scratch_shapes=[
            pltpu.VMEM((n_gx, 2, own_rows, width), BF16),
            pltpu.VMEM((2, total, width), BF16),
            pltpu.VMEM((2, slot_rows, width), F32),
            pltpu.VMEM((width, units), BF16),
            pltpu.VMEM((units, width), BF16),
            pltpu.VMEM((CHUNKS, n_gz, 2, r, units), F32),
            pltpu.VMEM((CHUNKS, n_hi, 2, r, units), F32),
            pltpu.VMEM((CHUNKS, 2, r, units), BF16),
            pltpu.VMEM((CHUNKS, 2, r, units), BF16),
            pltpu.VMEM((CHUNKS, 2, 2, r, units), BF16),
            pltpu.VMEM((CHUNKS, 2, 2, r, units), BF16),
            pltpu.VMEM((CHUNKS, n_gz, 2, r, units), BF16),
            pltpu.VMEM((total, width), BF16),
            pltpu.VMEM((n_gy, slot_rows, width), BF16),
            pltpu.VMEM((slot_rows, width), F32),
            pltpu.VMEM((n_gx, own_rows, width), BF16),
            pltpu.VMEM((n_gx, own_rows, width), BF16),
            dma((4,)),
            dma((n_gx,)),
            dma((n_gx,)),
            dma((2, n_gy // 2 + 1)),
            dma((2, n_gy // 2 + 1)),
            dma((CHUNKS, 5)),
            dma((CHUNKS, 5)),
            dma((CHUNKS, 4)),
            dma((CHUNKS, 4)),
            dma((CHUNKS, 4)),
            dma((CHUNKS, 4)),
            dma((n_gy,)),
            dma((n_gy,)),
            dma((n_gx,)),
            dma((n_gx,)),
        ],
        compiler_params=pltpu.CompilerParams(
            collective_id=0, has_side_effects=True, vmem_limit_bytes=48 * 1024 * 1024
        ),
    )(tokens, w_up, w_down, cotangent)


def solution(mesh):
    sizes = tuple(mesh.shape[axis] for axis in ("gx", "gy", "gz"))
    placed = (
        P(("gx", "gy"), "gz"),
        P("gz", ("gx", "gy")),
        P(("gx", "gy"), "gz"),
        P(("gx", "gy"), "gz"),
    )
    return jax.shard_map(
        functools.partial(on_device, sizes),
        mesh=mesh,
        in_specs=placed,
        out_specs=(P(("gx", "gy"), "gz"), P("gz", ("gx", "gy")), P(("gx", "gy"), "gz")),
        check_vma=False,
    )
```

```python
import functools
import math

import jax
import jax.numpy as jnp
from jax import lax
from jax.experimental import pallas as pl
from jax.experimental.pallas import tpu as pltpu
from jax.sharding import PartitionSpec as P

GELU_SCALE = math.sqrt(2.0 / math.pi)
CUBIC_COEFF = 0.044715
MESH = pl.DeviceIdType.MESH
BF16, F32 = jnp.bfloat16, jnp.float32
CHUNKS = 3


def activate(pre_act, back_grad):
    squared = pre_act * pre_act
    tangent = jnp.tanh(GELU_SCALE * pre_act * (1.0 + CUBIC_COEFF * squared))
    hidden = (0.5 * pre_act * (1.0 + tangent)).astype(BF16)
    gelu_slope = 0.5 * (1.0 + tangent) + 0.5 * pre_act * (1.0 - tangent * tangent) * GELU_SCALE * (
        1.0 + 3.0 * CUBIC_COEFF * squared
    )
    return hidden, (back_grad * gelu_slope).astype(BF16)


def slot_of(offset):
    return 0 if offset == 0 else 2 * offset - 1 if offset > 0 else -2 * offset


def dot_nt(a, b):
    return lax.dot_general(a, b, (((1,), (1,)), ((), ())), preferred_element_type=F32)


def dot_tn(a, b):
    return lax.dot_general(a, b, (((0,), (0,)), ((), ())), preferred_element_type=F32)


def kernel(
    sizes,
    tokens_ref, w_up_ref, w_down_ref, cot_ref,
    grad_in_ref, grad_up_ref, grad_down_ref,
    near, rows, wide, up, down, part, other, z1_out, z1_in, z2_out, z2_in, act,
    back, back_in, own48, last_out, last_in,
    local_sem, near_send, near_recv, y_send, y_recv, core_send, core_recv,
    z_send, z_recv, act_send, act_recv, back_send, back_recv, last_send, last_recv,
):
    n_gx, n_gy, n_gz = sizes
    n_hi = n_gz // 2
    own_rows = tokens_ref.shape[0]
    slot_rows = n_gx * own_rows
    total_rows = n_gy * slot_rows
    chunk_rows = total_rows // CHUNKS
    gx, gy, gz = lax.axis_index("gx"), lax.axis_index("gy"), lax.axis_index("gz")
    hi, core = gz // 2, gz % 2

    def at_gx(j):
        return ((gx + j) % n_gx, gy, gz)

    def at_gy(j):
        return (gx, (gy + n_gy + j) % n_gy, gz)

    def at_hi(j):
        return (gx, gy, ((hi + n_hi + j) % n_hi) * 2 + core)

    other_core = (gx, gy, hi * 2 + 1 - core)

    load_up = pltpu.make_async_copy(w_up_ref, up, local_sem.at[0])
    load_down = pltpu.make_async_copy(w_down_ref, down, local_sem.at[1])
    load_tokens = pltpu.make_async_copy(tokens_ref, near.at[gx, 0], local_sem.at[2])
    load_cot = pltpu.make_async_copy(cot_ref, near.at[gx, 1], local_sem.at[3])
    load_tokens.start()
    load_cot.start()
    load_up.start()
    load_down.start()

    partners = [at_gx(j) for j in range(1, n_gx)] + [at_gy(j) for j in range(1, n_gy)]
    partners += [at_hi(1), at_hi(-1), other_core]
    barrier = pltpu.get_barrier_semaphore()
    for partner in partners:
        pl.semaphore_signal(barrier, inc=1, device_id=partner, device_id_type=MESH)
    load_tokens.wait()
    load_cot.wait()
    pl.semaphore_wait(barrier, len(partners))

    sent = []

    def send(src, dst, send_sem, recv_sem, device):
        copy = pltpu.make_async_remote_copy(
            src_ref=src, dst_ref=dst, send_sem=send_sem, recv_sem=recv_sem, device_id=device, device_id_type=MESH
        )
        copy.start()
        sent.append(copy)

    def arrived(dst, recv_sem):
        pltpu.make_async_remote_copy(
            src_ref=dst, dst_ref=dst, send_sem=recv_sem, recv_sem=recv_sem, device_id=other_core, device_id_type=MESH
        ).wait_recv()

    for j in range(1, n_gx):
        send(near.at[gx], near.at[gx], near_send.at[j], near_recv.at[j], at_gx(j))
    for j in range(1, n_gx):
        arrived(near.at[(gx + n_gx - j) % n_gx], near_recv.at[j])
    for u in range(n_gx):
        for which in range(2):
            wide[which, u * own_rows : (u + 1) * own_rows] = near[u, which].astype(F32)
    rows[:, :slot_rows] = wide[...].astype(BF16)

    half = n_gy // 2
    split = slot_rows // 3 // 16 * 16

    def slot(which, offset, start=0, stop=slot_rows):
        first = slot_of(offset) * slot_rows
        return rows.at[which, first + start : first + stop]

    def hops(which, step):
        if step < half:
            lower = upper = (0, slot_rows)
        else:
            lower, upper = (0, split), (split, slot_rows)
        return (
            (slot(which, step - 1, *upper), slot(which, step, *upper), -1),
            (slot(which, 1 - step, *lower), slot(which, -step if step < half else half, *lower), 1),
        )

    def ring(which, step):
        for way, (src, dst, to) in enumerate(hops(which, step)):
            send(src, dst, y_send.at[way, which, step], y_recv.at[way, which, step], at_gy(to))

    def pass_on(step):
        for which in range(2):
            for way, (_, dst, _) in enumerate(hops(which, step)):
                arrived(dst, y_recv.at[way, which, step])
            if step < half:
                ring(which, step + 1)

    right, left, across = (hi + 1) % n_hi, (hi + n_hi - 1) % n_hi, (hi + 2) % n_hi

    def chunk(c):
        return pl.ds(c * chunk_rows, chunk_rows)

    def forward(c):
        for which, value in enumerate(
            (
                jnp.dot(rows[0, chunk(c)], up[...], preferred_element_type=F32),
                dot_nt(rows[1, chunk(c)], down[...]),
            )
        ):
            part[c, :, which] = value.reshape(n_gz, chunk_rows // n_gz, value.shape[1])
        theirs = part.at[c, pl.ds((1 - core) * n_hi, n_hi)]
        send(theirs, other.at[c], core_send.at[c, 0], core_recv.at[c, 0], other_core)

    def mine(c, h, which):
        return part[c, core * n_hi + h, which] + other[c, h, which]

    def z1(c):
        arrived(other.at[c], core_recv.at[c, 0])
        for which, to in ((0, 1), (1, -1)):
            z1_out[c, which] = mine(c, across, which).astype(BF16)
            send(z1_out.at[c, which], z1_in.at[c, which], z_send.at[c, which], z_recv.at[c, which], at_hi(to))

    def z2(c):
        arrived(z1_in.at[c, 0], z_recv.at[c, 0])
        z2_out[c, 0, 0] = (mine(c, right, 0) + z1_in[c, 0].astype(F32)).astype(BF16)
        z2_out[c, 0, 1] = mine(c, right, 1).astype(BF16)
        send(z2_out.at[c, 0], z2_in.at[c, 0], z_send.at[c, 2], z_recv.at[c, 2], at_hi(1))
        arrived(z1_in.at[c, 1], z_recv.at[c, 1])
        z2_out[c, 1, 0] = mine(c, left, 0).astype(BF16)
        z2_out[c, 1, 1] = (mine(c, left, 1) + z1_in[c, 1].astype(F32)).astype(BF16)
        send(z2_out.at[c, 1], z2_in.at[c, 1], z_send.at[c, 3], z_recv.at[c, 3], at_hi(-1))

    def held(c, h, k=core):
        return act.at[c, k * n_hi + h]

    def to_core(c, h, at):
        send(held(c, h), held(c, h), core_send.at[c, at], core_recv.at[c, at], other_core)

    def z3(c):
        arrived(z2_in.at[c, 0], z_recv.at[c, 2])
        arrived(z2_in.at[c, 1], z_recv.at[c, 3])
        pre_act, back_grad = (
            mine(c, hi, which) + z2_in[c, 0, which].astype(F32) + z2_in[c, 1, which].astype(F32) for which in range(2)
        )
        hidden, pre_grad = activate(pre_act, back_grad)
        act[c, gz % 2 * n_hi + hi, 0] = hidden
        act[c, gz % 2 * n_hi + hi, 1] = pre_grad
        send(held(c, hi), held(c, hi), act_send.at[c, 0], act_recv.at[c, 0], at_hi(1))
        send(held(c, hi), held(c, hi), act_send.at[c, 1], act_recv.at[c, 1], at_hi(-1))
        to_core(c, hi, 1)

    def z4(c):
        arrived(held(c, left), act_recv.at[c, 0])
        send(held(c, left).at[0], held(c, left).at[0], act_send.at[c, 2], act_recv.at[c, 2], at_hi(1))
        arrived(held(c, right), act_recv.at[c, 1])
        send(held(c, right).at[1], held(c, right).at[1], act_send.at[c, 3], act_recv.at[c, 3], at_hi(-1))
        to_core(c, left, 2)
        to_core(c, right, 3)

    def z5(c):
        arrived(held(c, across).at[0], act_recv.at[c, 2])
        arrived(held(c, across).at[1], act_recv.at[c, 3])
        to_core(c, across, 4)

    def z6(c):
        for at, h in ((1, hi), (2, left), (3, right), (4, across)):
            arrived(held(c, h, 1 - core), core_recv.at[c, at])

    def whole(c, which):
        return act[c, :, which].reshape(chunk_rows, act.shape[-1])

    tile = 16
    done = []

    def backward(c):
        value = dot_nt(whole(c, 1), up[...])
        first = c * chunk_rows
        back[first : first + chunk_rows] = value.astype(BF16)
        if c == 0:
            own48[...] = value[:slot_rows]
        for offset in range(1 - half, half + 1):
            at = slot_of(offset)
            if at and at not in done and (at + 1) * slot_rows <= first + chunk_rows:
                done.append(at)
                send(
                    back.at[at * slot_rows : (at + 1) * slot_rows], back_in.at[at],
                    back_send.at[at], back_recv.at[at], at_gy(offset),
                )

    ring(0, 1)
    ring(1, 1)
    load_up.wait()
    load_down.wait()
    pass_on(1)
    forward(0)
    pass_on(2)
    z1(0)
    pass_on(3)
    forward(1)
    z2(0)
    pass_on(4)
    z1(1)
    forward(2)
    z1(2)
    z3(0)
    z2(1)
    z2(2)
    z4(0)
    z3(1)
    z3(2)
    z5(0)
    z4(1)
    z6(0)
    backward(0)
    z4(2)
    z5(1)
    z6(1)
    backward(1)
    z5(2)
    z6(2)
    backward(2)

    hidden = jnp.concatenate([whole(c, 0) for c in range(CHUNKS)])
    pre_grad = jnp.concatenate([whole(c, 1) for c in range(CHUNKS)])
    grad_up_ref[...] = dot_tn(rows[0], pre_grad).astype(BF16)
    grad_down_ref[...] = dot_tn(hidden, rows[1]).astype(BF16)

    for at in range(1, n_gy):
        arrived(back_in.at[at], back_recv.at[at])
        own48[...] += back_in[at].astype(F32)
    for u in range(n_gx):
        last_out[u] = own48[u * own_rows : (u + 1) * own_rows].astype(BF16)
    for j in range(1, n_gx):
        send(last_out.at[(gx + j) % n_gx], last_in.at[j], last_send.at[j], last_recv.at[j], at_gx(j))
    result = last_out[gx].astype(F32)
    for j in range(1, n_gx):
        arrived(last_in.at[j], last_recv.at[j])
        result += last_in[j].astype(F32)
    grad_in_ref[...] = result
    for copy in sent:
        copy.wait_send()


def on_device(sizes, tokens, w_up, w_down, cotangent):
    n_gx, n_gy, n_gz = sizes
    own_rows, width = tokens.shape
    units = w_up.shape[1]
    slot_rows = n_gx * own_rows
    total = slot_rows * n_gy
    n_hi = n_gz // 2
    r = total // CHUNKS // n_gz
    dma = pltpu.SemaphoreType.DMA
    return pl.pallas_call(
        functools.partial(kernel, sizes),
        out_shape=(
            jax.ShapeDtypeStruct((own_rows, width), F32),
            jax.ShapeDtypeStruct((width, units), BF16),
            jax.ShapeDtypeStruct((units, width), BF16),
        ),
        in_specs=[pl.BlockSpec(memory_space=pltpu.HBM)] * 4,
        out_specs=(pl.BlockSpec(memory_space=pltpu.VMEM),) * 3,
        scratch_shapes=[
            pltpu.VMEM((n_gx, 2, own_rows, width), BF16),
            pltpu.VMEM((2, total, width), BF16),
            pltpu.VMEM((2, slot_rows, width), F32),
            pltpu.VMEM((width, units), BF16),
            pltpu.VMEM((units, width), BF16),
            pltpu.VMEM((CHUNKS, n_gz, 2, r, units), F32),
            pltpu.VMEM((CHUNKS, n_hi, 2, r, units), F32),
            pltpu.VMEM((CHUNKS, 2, r, units), BF16),
            pltpu.VMEM((CHUNKS, 2, r, units), BF16),
            pltpu.VMEM((CHUNKS, 2, 2, r, units), BF16),
            pltpu.VMEM((CHUNKS, 2, 2, r, units), BF16),
            pltpu.VMEM((CHUNKS, n_gz, 2, r, units), BF16),
            pltpu.VMEM((total, width), BF16),
            pltpu.VMEM((n_gy, slot_rows, width), BF16),
            pltpu.VMEM((slot_rows, width), F32),
            pltpu.VMEM((n_gx, own_rows, width), BF16),
            pltpu.VMEM((n_gx, own_rows, width), BF16),
            dma((4,)),
            dma((n_gx,)),
            dma((n_gx,)),
            dma((2, 2, n_gy // 2 + 1)),
            dma((2, 2, n_gy // 2 + 1)),
            dma((CHUNKS, 5)),
            dma((CHUNKS, 5)),
            dma((CHUNKS, 4)),
            dma((CHUNKS, 4)),
            dma((CHUNKS, 4)),
            dma((CHUNKS, 4)),
            dma((n_gy,)),
            dma((n_gy,)),
            dma((n_gx,)),
            dma((n_gx,)),
        ],
        compiler_params=pltpu.CompilerParams(
            collective_id=0, has_side_effects=True, vmem_limit_bytes=48 * 1024 * 1024
        ),
    )(tokens, w_up, w_down, cotangent)


def solution(mesh):
    sizes = tuple(mesh.shape[axis] for axis in ("gx", "gy", "gz"))
    placed = (
        P(("gx", "gy"), "gz"),
        P("gz", ("gx", "gy")),
        P(("gx", "gy"), "gz"),
        P(("gx", "gy"), "gz"),
    )
    return jax.shard_map(
        functools.partial(on_device, sizes),
        mesh=mesh,
        in_specs=placed,
        out_specs=(P(("gx", "gy"), "gz"), P("gz", ("gx", "gy")), P(("gx", "gy"), "gz")),
        check_vma=False,
    )
```

```python
import functools
import math

import jax
import jax.numpy as jnp
from jax import lax
from jax.experimental import pallas as pl
from jax.experimental.pallas import tpu as pltpu
from jax.sharding import PartitionSpec as P

GELU_SCALE = math.sqrt(2.0 / math.pi)
CUBIC_COEFF = 0.044715
MESH = pl.DeviceIdType.MESH
BF16, F32 = jnp.bfloat16, jnp.float32
CHUNKS = 3
PIECES = 3
VMEM_LIMIT = 63 * 1024 * 1024
N_X = 4


def activate(pre_act, back_grad):
    squared = pre_act * pre_act
    tangent = jnp.tanh(GELU_SCALE * pre_act * (1.0 + CUBIC_COEFF * squared))
    hidden = (0.5 * pre_act * (1.0 + tangent)).astype(BF16)
    gelu_slope = 0.5 * (1.0 + tangent) + 0.5 * pre_act * (1.0 - tangent * tangent) * GELU_SCALE * (
        1.0 + 3.0 * CUBIC_COEFF * squared
    )
    return hidden, (back_grad * gelu_slope).astype(BF16)


def slot_of(offset):
    return 0 if offset == 0 else 2 * offset - 1 if offset > 0 else -2 * offset


def dot_nt(a, b):
    return lax.dot_general(a, b, (((1,), (1,)), ((), ())), preferred_element_type=F32)


def dot_tn(a, b):
    return lax.dot_general(a, b, (((0,), (0,)), ((), ())), preferred_element_type=F32)


def kernel(
    sizes,
    tokens_ref, w_up_ref, w_down_ref, cot_ref,
    grad_in_ref, grad_up_ref, grad_down_ref,
    near, rows, wide, up, down, part, other, act,
    pair_sum, pair_out, pair_in, back, x_out, x_in, back_out, back_in, own_sum, last_out, last_in, grad_up, grad_down,
    local_sem, near_send, near_recv, y_send, y_recv, core_send, core_recv,
    z_send, z_recv, x_send, x_recv, back_send, back_recv, last_send, last_recv,
):
    n_gx, n_gy, n_gz = sizes
    n_hi = n_gz // 2
    own_rows = tokens_ref.shape[0]
    slot_rows = n_gx * own_rows
    total_rows = n_gy * slot_rows
    chunk_rows = total_rows // CHUNKS
    gx, gy, gz = lax.axis_index("gx"), lax.axis_index("gy"), lax.axis_index("gz")
    hi, core = gz // 2, gz % 2
    n_low = n_gx // N_X
    at_x, low = gx // n_low, gx % n_low

    def at_gx(j):
        return ((at_x + j // n_low) % N_X * n_low + (low + j % n_low) % n_low, gy, gz)

    def at_gy(j):
        return (gx, (gy + n_gy + j) % n_gy, gz)

    def at_hi(j):
        return (gx, gy, ((hi + n_hi + j) % n_hi) * 2 + core)

    other_core = (gx, gy, hi * 2 + 1 - core)

    load_up = pltpu.make_async_copy(w_up_ref, up, local_sem.at[0])
    load_down = pltpu.make_async_copy(w_down_ref, down, local_sem.at[1])
    load_tokens = pltpu.make_async_copy(tokens_ref, near.at[0, 0], local_sem.at[2])
    load_cot = pltpu.make_async_copy(cot_ref, near.at[0, 1], local_sem.at[3])
    load_tokens.start()
    load_cot.start()
    load_up.start()
    load_down.start()

    partners = [at_gx(j) for j in range(1, n_gx)] + [at_gy(j) for j in range(1, n_gy)]
    partners += [at_hi(1), at_hi(-1), other_core]
    barrier = pltpu.get_barrier_semaphore()
    for partner in partners:
        pl.semaphore_signal(barrier, inc=1, device_id=partner, device_id_type=MESH)
    load_tokens.wait()
    load_cot.wait()
    pl.semaphore_wait(barrier, len(partners))

    sent = []

    def send(src, dst, send_sem, recv_sem, device):
        copy = pltpu.make_async_remote_copy(
            src_ref=src, dst_ref=dst, send_sem=send_sem, recv_sem=recv_sem, device_id=device, device_id_type=MESH
        )
        copy.start()
        sent.append(copy)

    def arrived(dst, recv_sem):
        pltpu.make_async_remote_copy(
            src_ref=dst, dst_ref=dst, send_sem=recv_sem, recv_sem=recv_sem, device_id=other_core, device_id_type=MESH
        ).wait_recv()

    for j in range(1, n_gx):
        send(near.at[0], near.at[j], near_send.at[j], near_recv.at[j], at_gx(j))
    for j in range(n_gx):
        if j:
            arrived(near.at[j], near_recv.at[j])
        for which in range(2):
            wide[which, j * own_rows : (j + 1) * own_rows] = near[j, which].astype(F32)
    rows[:, :slot_rows] = wide[...].astype(BF16)

    half = n_gy // 2
    piece = slot_rows // PIECES

    def hop(step, which, at, way):
        offset = step if way == 0 or step == half else -step
        before = step - 1 if way == 0 else 1 - step
        src, dst = (slot_of(o) * slot_rows + at * piece for o in (before, offset))
        return rows.at[which, src : src + piece], rows.at[which, dst : dst + piece]

    def travels(step, which, way):
        return step < half or which == way

    def ring(step, which, at, way):
        src, dst = hop(step, which, at, way)
        sems = (way, which, at, step)
        send(src, dst, y_send.at[sems], y_recv.at[sems], at_gy(-1 if way == 0 else 1))

    order = [(which, at, way) for at in range(PIECES) for which in range(2) for way in range(2)]

    def pass_on(step):
        for which, at, way in order:
            if step and travels(step, which, way):
                arrived(hop(step, which, at, way)[1], y_recv.at[way, which, at, step])
            if step < half and travels(step + 1, which, way):
                ring(step + 1, which, at, way)

    def chunk(c):
        return pl.ds(c * chunk_rows, chunk_rows)

    def forward(c):
        for which, value in enumerate(
            (
                jnp.dot(rows[0, chunk(c)], up[...], preferred_element_type=F32),
                dot_nt(rows[1, chunk(c)], down[...]),
            )
        ):
            part[c, :, which] = value.reshape(n_gz, chunk_rows // n_gz, value.shape[1])
        theirs = part.at[c, pl.ds((1 - core) * n_hi, n_hi)]
        send(theirs, other.at[c], core_send.at[c, 0], core_recv.at[c, 0], other_core)

    towards = 1 - 2 * (hi % 2)

    def pair_send(c, step, which):
        pair_out[c, step, which] = pair_sum[c, which].astype(BF16)
        to = towards if (step + which) % 2 == 0 else -towards
        send(
            pair_out.at[c, step, which], pair_in.at[c, step, which],
            z_send.at[c, 2 * step + which], z_recv.at[c, 2 * step + which], at_hi(to),
        )

    def pair_add(c, step, which):
        arrived(pair_in.at[c, step, which], z_recv.at[c, 2 * step + which])
        pair_sum[c, which] += pair_in[c, step, which].astype(F32)

    def e1(c):
        arrived(other.at[c], core_recv.at[c, 0])
        for which in range(2):
            pair_sum[c, which] = part[c, pl.ds(core * n_hi, n_hi), which] + other[c, :, which]
            pair_send(c, 0, which)

    def e2(c):
        for which in range(2):
            pair_add(c, 0, which)
            pair_send(c, 1, which)

    def e3(c):
        for which in range(2):
            pair_add(c, 1, which)
        hidden, pre_grad = activate(pair_sum[c, 0], pair_sum[c, 1])
        act[c, pl.ds(core * n_hi, n_hi), 0] = hidden
        act[c, pl.ds(core * n_hi, n_hi), 1] = pre_grad
        mine_all = act.at[c, pl.ds(core * n_hi, n_hi)]
        send(mine_all, mine_all, core_send.at[c, 1], core_recv.at[c, 1], other_core)

    def e6(c):
        arrived(act.at[c, pl.ds((1 - core) * n_hi, n_hi)], core_recv.at[c, 1])

    def whole(c, which):
        return act[c, :, which].reshape(chunk_rows, act.shape[-1])

    x_rows = slot_rows // N_X
    slots = {slot_of(offset): offset for offset in range(1 - half, half + 1)}

    def finished(c):
        return [at for at in slots if c * chunk_rows < (at + 1) * slot_rows <= (c + 1) * chunk_rows]

    def group(at, j):
        start = at * slot_rows + j * x_rows
        return back[start : start + x_rows]

    def backward(c):
        first = c * chunk_rows
        back[first : first + chunk_rows] = dot_nt(whole(c, 1), up[...])
        done = sorted(finished(c))
        for j in range(1, N_X):
            for i, at in enumerate(done):
                x_out[c, j, i] = group(at, j).astype(BF16)
            send(
                x_out.at[c, j, pl.ds(0, len(done))], x_in.at[c, j, pl.ds(0, len(done))],
                x_send.at[c, j], x_recv.at[c, j], at_gx((N_X - j) * n_low),
            )

    def sum_x(c):
        done = sorted(finished(c))
        for j in range(1, N_X):
            arrived(x_in.at[c, j, pl.ds(0, len(done))], x_recv.at[c, j])
        for i, at in enumerate(done):
            total = group(at, 0)
            for j in range(1, N_X):
                total += x_in[c, j, i].astype(F32)
            if at == 0:
                own_sum[...] = total
            else:
                back_out[at] = total.astype(BF16)
                send(back_out.at[at], back_in.at[at], back_send.at[at], back_recv.at[at], at_gy(slots[at]))

    pass_on(0)
    load_up.wait()
    load_down.wait()
    pass_on(1)
    forward(0)
    pass_on(2)
    e1(0)
    pass_on(3)
    forward(1)
    pass_on(4)
    e1(1)
    forward(2)
    e2(0)
    e1(2)
    e2(1)
    e3(0)
    e2(2)
    e6(0)
    backward(0)
    e3(1)
    e6(1)
    backward(1)
    e3(2)
    sum_x(0)
    e6(2)
    backward(2)
    sum_x(1)
    sum_x(2)

    hidden = jnp.concatenate([whole(c, 0) for c in range(CHUNKS)])
    pre_grad = jnp.concatenate([whole(c, 1) for c in range(CHUNKS)])
    grad_up[...] = dot_tn(rows[0], pre_grad).astype(BF16)
    store_up = pltpu.make_async_copy(grad_up, grad_up_ref, local_sem.at[0])
    store_up.start()
    grad_down[...] = dot_tn(hidden, rows[1]).astype(BF16)
    store_down = pltpu.make_async_copy(grad_down, grad_down_ref, local_sem.at[1])
    store_down.start()

    for at in range(1, n_gy):
        arrived(back_in.at[at], back_recv.at[at])
        own_sum[...] += back_in[at].astype(F32)
    for j in range(1, n_low):
        last_out[j] = own_sum[j * own_rows : (j + 1) * own_rows].astype(BF16)
        send(last_out.at[j], last_in.at[j], last_send.at[j], last_recv.at[j], at_gx(n_low - j))
    result = own_sum[:own_rows]
    for j in range(1, n_low):
        arrived(last_in.at[j], last_recv.at[j])
        result += last_in[j].astype(F32)
    grad_in_ref[...] = result
    store_up.wait()
    store_down.wait()
    for copy in sent:
        copy.wait_send()


def hand_over(*refs):
    for src, dst in zip(refs[:3], refs[3:]):
        dst[...] = src[...]


def on_device(sizes, tokens, w_up, w_down, cotangent):
    n_gx, n_gy, n_gz = sizes
    own_rows, width = tokens.shape
    units = w_up.shape[1]
    slot_rows = n_gx * own_rows
    total = slot_rows * n_gy
    n_hi = n_gz // 2
    r = total // CHUNKS // n_gz
    n_low, x_rows = n_gx // N_X, slot_rows // N_X
    dma = pltpu.SemaphoreType.DMA
    results = pl.pallas_call(
        functools.partial(kernel, sizes),
        out_shape=(
            jax.ShapeDtypeStruct((own_rows, width), F32),
            jax.ShapeDtypeStruct((width, units), BF16),
            jax.ShapeDtypeStruct((units, width), BF16),
        ),
        in_specs=[pl.BlockSpec(memory_space=pltpu.HBM)] * 4,
        out_specs=(
            pl.BlockSpec(memory_space=pltpu.VMEM),
            pl.BlockSpec(memory_space=pl.ANY),
            pl.BlockSpec(memory_space=pl.ANY),
        ),
        scratch_shapes=[
            pltpu.VMEM((n_gx, 2, own_rows, width), BF16),
            pltpu.VMEM((2, total, width), BF16),
            pltpu.VMEM((2, slot_rows, width), F32),
            pltpu.VMEM((width, units), BF16),
            pltpu.VMEM((units, width), BF16),
            pltpu.VMEM((CHUNKS, n_gz, 2, r, units), F32),
            pltpu.VMEM((CHUNKS, n_hi, 2, r, units), F32),
            pltpu.VMEM((CHUNKS, n_gz, 2, r, units), BF16),
            pltpu.VMEM((CHUNKS, 2, n_hi, r, units), F32),
            pltpu.VMEM((CHUNKS, 2, 2, n_hi, r, units), BF16),
            pltpu.VMEM((CHUNKS, 2, 2, n_hi, r, units), BF16),
            pltpu.VMEM((total, width), F32),
            pltpu.VMEM((CHUNKS, N_X, n_gy // 2, x_rows, width), BF16),
            pltpu.VMEM((CHUNKS, N_X, n_gy // 2, x_rows, width), BF16),
            pltpu.VMEM((n_gy, x_rows, width), BF16),
            pltpu.VMEM((n_gy, x_rows, width), BF16),
            pltpu.VMEM((x_rows, width), F32),
            pltpu.VMEM((n_low, own_rows, width), BF16),
            pltpu.VMEM((n_low, own_rows, width), BF16),
            pltpu.VMEM((width, units), BF16),
            pltpu.VMEM((units, width), BF16),
            dma((4,)),
            dma((n_gx,)),
            dma((n_gx,)),
            dma((2, 2, PIECES, n_gy // 2 + 1)),
            dma((2, 2, PIECES, n_gy // 2 + 1)),
            dma((CHUNKS, 2)),
            dma((CHUNKS, 2)),
            dma((CHUNKS, 4)),
            dma((CHUNKS, 4)),
            dma((CHUNKS, N_X)),
            dma((CHUNKS, N_X)),
            dma((n_gy,)),
            dma((n_gy,)),
            dma((n_gx // N_X,)),
            dma((n_gx // N_X,)),
        ],
        compiler_params=pltpu.CompilerParams(
            collective_id=0, has_side_effects=True, vmem_limit_bytes=VMEM_LIMIT
        ),
    )(tokens, w_up, w_down, cotangent)
    return pl.pallas_call(
        hand_over,
        out_shape=tuple(jax.ShapeDtypeStruct(a.shape, a.dtype) for a in results),
        in_specs=[pl.BlockSpec(memory_space=pltpu.VMEM)] * 3,
        out_specs=(pl.BlockSpec(memory_space=pltpu.VMEM),) * 3,
        compiler_params=pltpu.CompilerParams(vmem_limit_bytes=VMEM_LIMIT),
    )(*results)


def solution(mesh):
    sizes = tuple(mesh.shape[axis] for axis in ("gx", "gy", "gz"))
    placed = (
        P(("gx", "gy"), "gz"),
        P("gz", ("gx", "gy")),
        P(("gx", "gy"), "gz"),
        P(("gx", "gy"), "gz"),
    )
    return jax.shard_map(
        functools.partial(on_device, sizes),
        mesh=mesh,
        in_specs=placed,
        out_specs=(P(("gx", "gy"), "gz"), P("gz", ("gx", "gy")), P(("gx", "gy"), "gz")),
        check_vma=False,
    )
```

```python
import functools
import math

import jax
import jax.numpy as jnp
from jax import lax
from jax.experimental import pallas as pl
from jax.experimental.pallas import tpu as pltpu
from jax.sharding import PartitionSpec as P

GELU_SCALE = math.sqrt(2.0 / math.pi)
CUBIC_COEFF = 0.044715
MESH = pl.DeviceIdType.MESH
BF16, F32 = jnp.bfloat16, jnp.float32
CHUNKS = 3
PIECES = 3
VMEM_LIMIT = 63 * 1024 * 1024
N_X = 4


def activate(pre_act, back_grad):
    squared = pre_act * pre_act
    tangent = jnp.tanh(GELU_SCALE * pre_act * (1.0 + CUBIC_COEFF * squared))
    hidden = (0.5 * pre_act * (1.0 + tangent)).astype(BF16)
    gelu_slope = 0.5 * (1.0 + tangent) + 0.5 * pre_act * (1.0 - tangent * tangent) * GELU_SCALE * (
        1.0 + 3.0 * CUBIC_COEFF * squared
    )
    return hidden, (back_grad * gelu_slope).astype(BF16)


def slot_of(offset):
    return 0 if offset == 0 else 2 * offset - 1 if offset > 0 else -2 * offset


def dot_nt(a, b):
    return lax.dot_general(a, b, (((1,), (1,)), ((), ())), preferred_element_type=F32)


def dot_tn(a, b):
    return lax.dot_general(a, b, (((0,), (0,)), ((), ())), preferred_element_type=F32)


def kernel(
    sizes,
    tokens_ref, w_up_ref, w_down_ref, cot_ref,
    grad_in_ref, grad_up_ref, grad_down_ref,
    near, far, rows, wide, up, down, up_t, down_t, part, other, act,
    pair_sum, pair_out, pair_in, back, x_out, x_in, back_out, back_in, own_sum, last_out, last_in, grad_up, grad_down,
    local_sem, near_send, near_recv, far_send, far_recv, y_send, y_recv, core_send, core_recv,
    z_send, z_recv, x_send, x_recv, back_send, back_recv, last_send, last_recv,
):
    n_gx, n_gy, n_gz = sizes
    n_hi = n_gz // 2
    own_rows = tokens_ref.shape[0]
    slot_rows = n_gx * own_rows
    total_rows = n_gy * slot_rows
    chunk_rows = total_rows // CHUNKS
    gx, gy, gz = lax.axis_index("gx"), lax.axis_index("gy"), lax.axis_index("gz")
    hi, core = gz // 2, gz % 2
    n_low = n_gx // N_X
    at_x, low = gx // n_low, gx % n_low

    def at_gx(j):
        return ((at_x + j // n_low) % N_X * n_low + (low + j % n_low) % n_low, gy, gz)

    def at_gy(j):
        return (gx, (gy + n_gy + j) % n_gy, gz)

    def at_hi(j):
        return (gx, gy, ((hi + n_hi + j) % n_hi) * 2 + core)

    other_core = (gx, gy, hi * 2 + 1 - core)

    load_up = pltpu.make_async_copy(w_up_ref, up, local_sem.at[0])
    load_down = pltpu.make_async_copy(w_down_ref, down, local_sem.at[1])
    load_tokens = pltpu.make_async_copy(tokens_ref, near.at[0, 0], local_sem.at[2])
    load_cot = pltpu.make_async_copy(cot_ref, near.at[0, 1], local_sem.at[3])
    load_tokens.start()
    load_cot.start()
    load_up.start()
    load_down.start()

    partners = [at_gx(j) for j in range(1, n_gx)] + [at_gy(j) for j in range(1, n_gy)]
    partners += [at_hi(1), at_hi(-1), other_core]
    barrier = pltpu.get_barrier_semaphore()
    for partner in partners:
        pl.semaphore_signal(barrier, inc=1, device_id=partner, device_id_type=MESH)
    load_tokens.wait()
    load_cot.wait()
    pl.semaphore_wait(barrier, len(partners))

    sent = []

    def send(src, dst, send_sem, recv_sem, device):
        copy = pltpu.make_async_remote_copy(
            src_ref=src, dst_ref=dst, send_sem=send_sem, recv_sem=recv_sem, device_id=device, device_id_type=MESH
        )
        copy.start()
        sent.append(copy)

    def arrived(dst, recv_sem):
        pltpu.make_async_remote_copy(
            src_ref=dst, dst_ref=dst, send_sem=recv_sem, recv_sem=recv_sem, device_id=other_core, device_id_type=MESH
        ).wait_recv()

    for j in range(1, n_gx):
        send(near.at[0], near.at[j], near_send.at[j], near_recv.at[j], at_gx(j))
    send(near.at[0], far.at[0], far_send.at[0], far_recv.at[0], at_gy(n_gy // 2))
    load_up.wait()
    load_down.wait()
    down_t[...] = down[...].T
    up_t[...] = up[...].T
    for j in range(n_gx):
        if j:
            arrived(near.at[j], near_recv.at[j])
        for which in range(2):
            wide[which, j * own_rows : (j + 1) * own_rows] = near[j, which].astype(F32)
    rows[:, :slot_rows] = wide[...].astype(BF16)

    def far_low():
        arrived(far.at[0], far_recv.at[0])
        for j in range(1, n_low):
            send(far.at[0], far.at[j], far_send.at[j], far_recv.at[j], at_gx(j))

    def far_x():
        for j in range(1, n_low):
            arrived(far.at[j], far_recv.at[j])
        for j in range(1, N_X):
            group = pl.ds(j * n_low, n_low)
            send(
                far.at[pl.ds(0, n_low)], far.at[group],
                far_send.at[n_low + j], far_recv.at[n_low + j], at_gx(j * n_low),
            )

    def far_rows():
        for j in range(N_X):
            if j:
                arrived(far.at[pl.ds(j * n_low, n_low)], far_recv.at[n_low + j])
            for k in range(j * n_low, (j + 1) * n_low):
                for which in range(2):
                    wide[which, k * own_rows : (k + 1) * own_rows] = far[k, which].astype(F32)
        first = slot_of(half) * slot_rows
        rows[:, first : first + slot_rows] = wide[...].astype(BF16)

    half = n_gy // 2
    piece = slot_rows // PIECES

    def hop(step, which, at, way):
        offsets = (step - 1, step) if way == 0 else (1 - step, -step)
        src, dst = (slot_of(o) * slot_rows + at * piece for o in offsets)
        return rows.at[which, src : src + piece], rows.at[which, dst : dst + piece]

    def ring(step, which, at, way):
        src, dst = hop(step, which, at, way)
        sems = (way, which, at, step)
        send(src, dst, y_send.at[sems], y_recv.at[sems], at_gy(-1 if way == 0 else 1))

    order = [(which, at, way) for at in range(PIECES) for which in range(2) for way in range(2)]

    def pass_on(step):
        for which, at, way in order:
            if step:
                arrived(hop(step, which, at, way)[1], y_recv.at[way, which, at, step])
            if step < half - 1:
                ring(step + 1, which, at, way)

    def chunk(c):
        return pl.ds(c * chunk_rows, chunk_rows)

    def forward(c):
        for which, value in enumerate(
            (
                jnp.dot(rows[0, chunk(c)], up[...], preferred_element_type=F32),
                jnp.dot(rows[1, chunk(c)], down_t[...], preferred_element_type=F32),
            )
        ):
            part[c, :, which] = value.reshape(n_gz, chunk_rows // n_gz, value.shape[1])
        theirs = part.at[c, pl.ds((1 - core) * n_hi, n_hi)]
        send(theirs, other.at[c], core_send.at[c, 0], core_recv.at[c, 0], other_core)

    towards = 1 - 2 * (hi % 2)
    partner = (at_hi(towards), at_hi(-towards))
    kept = ((hi // 2 + hi % 2) % 2, 2 + hi // 2)
    given = (1 - kept[0], 5 - kept[1])

    def chip_sum(c, tile):
        return part[c, core * n_hi + tile] + other[c, tile]

    def pair_send(c, step, which, to):
        at = (c, step, which)
        send(pair_out.at[at], pair_in.at[at], z_send.at[at], z_recv.at[at], partner[to])

    def pair_add(c, step, which):
        at = (c, step, which)
        arrived(pair_in.at[at], z_recv.at[at])
        pair_sum[c, which] += pair_in[at].astype(F32)

    def tile_of(c, tile, of=core):
        return act.at[c, of * n_hi + tile]

    def to_core(c, tile, at):
        send(tile_of(c, tile), tile_of(c, tile), core_send.at[c, at], core_recv.at[c, at], other_core)

    def e1(c):
        arrived(other.at[c], core_recv.at[c, 0])
        for which in range(2):
            pair_out[c, 0, which] = chip_sum(c, given[which]).astype(BF16)
            pair_send(c, 0, which, which)
        for which in range(2):
            pair_sum[c, which] = chip_sum(c, kept[which])

    def e2(c):
        for which in range(2):
            pair_add(c, 0, which)
            pair_out[c, 1, which] = pair_sum[c, which].astype(BF16)
            pair_send(c, 1, which, 1 - which)

    def e3(c):
        for which in range(2):
            pair_add(c, 1, which)
            hidden, pre_grad = activate(pair_sum[c, which, 0], pair_sum[c, which, 1])
            act[c, core * n_hi + kept[which], 0] = hidden
            act[c, core * n_hi + kept[which], 1] = pre_grad
            tile = tile_of(c, kept[which])
            send(tile, tile, z_send.at[c, 2, which], z_recv.at[c, 2, which], partner[which])
            to_core(c, kept[which], 1 + which)

    def e4(c):
        for which in range(2):
            arrived(tile_of(c, given[which]), z_recv.at[c, 2, which])
            to_core(c, given[which], 3 + which)

    def e6(c):
        for which in range(2):
            arrived(tile_of(c, kept[which], 1 - core), core_recv.at[c, 1 + which])
            arrived(tile_of(c, given[which], 1 - core), core_recv.at[c, 3 + which])

    def whole(c, which):
        return act[c, :, which].reshape(chunk_rows, act.shape[-1])

    x_rows = slot_rows // N_X
    slots = {slot_of(offset): offset for offset in range(1 - half, half + 1)}

    def finished(c):
        return [at for at in slots if c * chunk_rows < (at + 1) * slot_rows <= (c + 1) * chunk_rows]

    def group(at, j):
        start = at * slot_rows + j * x_rows
        return back[start : start + x_rows]

    def backward(c):
        first = c * chunk_rows
        back[first : first + chunk_rows] = jnp.dot(whole(c, 1), up_t[...], preferred_element_type=F32)
        done = sorted(finished(c))
        for j in range(1, N_X):
            for i, at in enumerate(done):
                x_out[c, j, i] = group(at, j).astype(BF16)
            send(
                x_out.at[c, j, pl.ds(0, len(done))], x_in.at[c, j, pl.ds(0, len(done))],
                x_send.at[c, j], x_recv.at[c, j], at_gx((N_X - j) * n_low),
            )

    def sum_x(c):
        done = sorted(finished(c))
        for j in range(1, N_X):
            arrived(x_in.at[c, j, pl.ds(0, len(done))], x_recv.at[c, j])
        for i, at in enumerate(done):
            total = group(at, 0)
            for j in range(1, N_X):
                total += x_in[c, j, i].astype(F32)
            if at == 0:
                own_sum[...] = total
            else:
                back_out[at] = total.astype(BF16)
                send(back_out.at[at], back_in.at[at], back_send.at[at], back_recv.at[at], at_gy(slots[at]))

    stores = (
        pltpu.make_async_copy(grad_up, grad_up_ref, local_sem.at[0]),
        pltpu.make_async_copy(grad_down, grad_down_ref, local_sem.at[1]),
    )

    def weights():
        hidden = jnp.concatenate([whole(c, 0) for c in range(CHUNKS)])
        pre_grad = jnp.concatenate([whole(c, 1) for c in range(CHUNKS)])
        grad_up[...] = dot_tn(rows[0], pre_grad).astype(BF16)
        stores[0].start()
        grad_down[...] = dot_tn(hidden, rows[1]).astype(BF16)
        stores[1].start()

    pass_on(0)
    far_low()
    pass_on(1)
    far_x()
    forward(0)
    pass_on(2)
    e1(0)
    far_rows()
    pass_on(3)
    forward(1)
    e1(1)
    forward(2)
    e2(0)
    e1(2)
    e2(1)
    e3(0)
    e2(2)
    e3(1)
    e4(0)
    e3(2)
    e6(0)
    backward(0)
    e4(1)
    e6(1)
    backward(1)
    sum_x(0)
    e4(2)
    e6(2)
    backward(2)
    sum_x(1)
    sum_x(2)
    weights()

    for at in range(1, n_gy):
        arrived(back_in.at[at], back_recv.at[at])
        own_sum[...] += back_in[at].astype(F32)
    for j in range(1, n_low):
        last_out[j] = own_sum[j * own_rows : (j + 1) * own_rows].astype(BF16)
        send(last_out.at[j], last_in.at[j], last_send.at[j], last_recv.at[j], at_gx(n_low - j))
    result = own_sum[:own_rows]
    for j in range(1, n_low):
        arrived(last_in.at[j], last_recv.at[j])
        result += last_in[j].astype(F32)
    grad_in_ref[...] = result
    for store in stores:
        store.wait()
    for copy in sent:
        copy.wait_send()


def hand_over(*refs):
    buffers, (loaded, stored) = refs[6:9], refs[9:]
    loads, stores = [], []
    for src, held, dst in zip(refs[:3], buffers, refs[3:6]):
        parts = 4 if src.shape[0] % 64 == 0 else 1
        size = src.shape[0] // parts
        for p in range(parts):
            part, n = pl.ds(p * size, size), len(loads)
            loads.append(pltpu.make_async_copy(src.at[part], held.at[part], loaded.at[n]))
            stores.append(pltpu.make_async_copy(held.at[part], dst.at[part], stored.at[n]))
    for load in loads:
        load.start()
    for load, store in zip(loads, stores):
        load.wait()
        store.start()
    for store in stores:
        store.wait()


def on_device(sizes, tokens, w_up, w_down, cotangent):
    n_gx, n_gy, n_gz = sizes
    own_rows, width = tokens.shape
    units = w_up.shape[1]
    slot_rows = n_gx * own_rows
    total = slot_rows * n_gy
    n_hi = n_gz // 2
    r = total // CHUNKS // n_gz
    n_low, x_rows = n_gx // N_X, slot_rows // N_X
    dma = pltpu.SemaphoreType.DMA
    results = pl.pallas_call(
        functools.partial(kernel, sizes),
        out_shape=(
            jax.ShapeDtypeStruct((own_rows, width), F32),
            jax.ShapeDtypeStruct((width, units), BF16),
            jax.ShapeDtypeStruct((units, width), BF16),
        ),
        in_specs=[pl.BlockSpec(memory_space=pltpu.HBM)] * 4,
        out_specs=(
            pl.BlockSpec(memory_space=pltpu.VMEM),
            pl.BlockSpec(memory_space=pl.ANY),
            pl.BlockSpec(memory_space=pl.ANY),
        ),
        scratch_shapes=[
            pltpu.VMEM((n_gx, 2, own_rows, width), BF16),
            pltpu.VMEM((n_gx, 2, own_rows, width), BF16),
            pltpu.VMEM((2, total, width), BF16),
            pltpu.VMEM((2, slot_rows, width), F32),
            pltpu.VMEM((width, units), BF16),
            pltpu.VMEM((units, width), BF16),
            pltpu.VMEM((units, width), BF16),
            pltpu.VMEM((width, units), BF16),
            pltpu.VMEM((CHUNKS, n_gz, 2, r, units), F32),
            pltpu.VMEM((CHUNKS, n_hi, 2, r, units), F32),
            pltpu.VMEM((CHUNKS, n_gz, 2, r, units), BF16),
            pltpu.VMEM((CHUNKS, 2, 2, r, units), F32),
            pltpu.VMEM((CHUNKS, 2, 2, 2, r, units), BF16),
            pltpu.VMEM((CHUNKS, 2, 2, 2, r, units), BF16),
            pltpu.VMEM((total, width), F32),
            pltpu.VMEM((CHUNKS, N_X, n_gy // 2, x_rows, width), BF16),
            pltpu.VMEM((CHUNKS, N_X, n_gy // 2, x_rows, width), BF16),
            pltpu.VMEM((n_gy, x_rows, width), BF16),
            pltpu.VMEM((n_gy, x_rows, width), BF16),
            pltpu.VMEM((x_rows, width), F32),
            pltpu.VMEM((n_low, own_rows, width), BF16),
            pltpu.VMEM((n_low, own_rows, width), BF16),
            pltpu.VMEM((width, units), BF16),
            pltpu.VMEM((units, width), BF16),
            dma((4,)),
            dma((n_gx,)),
            dma((n_gx,)),
            dma((n_low + N_X,)),
            dma((n_low + N_X,)),
            dma((2, 2, PIECES, n_gy // 2 + 1)),
            dma((2, 2, PIECES, n_gy // 2 + 1)),
            dma((CHUNKS, 5)),
            dma((CHUNKS, 5)),
            dma((CHUNKS, 3, 2)),
            dma((CHUNKS, 3, 2)),
            dma((CHUNKS, N_X)),
            dma((CHUNKS, N_X)),
            dma((n_gy,)),
            dma((n_gy,)),
            dma((n_gx // N_X,)),
            dma((n_gx // N_X,)),
        ],
        compiler_params=pltpu.CompilerParams(
            collective_id=0, has_side_effects=True, vmem_limit_bytes=VMEM_LIMIT
        ),
    )(tokens, w_up, w_down, cotangent)
    return pl.pallas_call(
        hand_over,
        out_shape=tuple(jax.ShapeDtypeStruct(a.shape, a.dtype) for a in results),
        in_specs=[pl.BlockSpec(memory_space=pl.ANY)] * 3,
        out_specs=(pl.BlockSpec(memory_space=pl.ANY),) * 3,
        scratch_shapes=[pltpu.VMEM(a.shape, a.dtype) for a in results] + [dma((9,)), dma((9,))],
        compiler_params=pltpu.CompilerParams(vmem_limit_bytes=VMEM_LIMIT),
    )(*results)


def solution(mesh):
    sizes = tuple(mesh.shape[axis] for axis in ("gx", "gy", "gz"))
    placed = (
        P(("gx", "gy"), "gz"),
        P("gz", ("gx", "gy")),
        P(("gx", "gy"), "gz"),
        P(("gx", "gy"), "gz"),
    )
    return jax.shard_map(
        functools.partial(on_device, sizes),
        mesh=mesh,
        in_specs=placed,
        out_specs=(P(("gx", "gy"), "gz"), P("gz", ("gx", "gy")), P(("gx", "gy"), "gz")),
        check_vma=False,
    )
```

```python
import functools
import math

import jax
import jax.numpy as jnp
from jax import lax
from jax.experimental import pallas as pl
from jax.experimental.pallas import tpu as pltpu
from jax.sharding import PartitionSpec as P

GELU_SCALE = math.sqrt(2.0 / math.pi)
CUBIC_COEFF = 0.044715
MESH = pl.DeviceIdType.MESH
BF16, F32 = jnp.bfloat16, jnp.float32
CHUNKS = 3
PIECES = 3
FAR = (3, -3, 4)
STEPS = 2
VMEM_LIMIT = 63 * 1024 * 1024
N_X = 4


def activate(pre_act, back_grad):
    squared = pre_act * pre_act
    tangent = jnp.tanh(GELU_SCALE * pre_act * (1.0 + CUBIC_COEFF * squared))
    hidden = (0.5 * pre_act * (1.0 + tangent)).astype(BF16)
    gelu_slope = 0.5 * (1.0 + tangent) + 0.5 * pre_act * (1.0 - tangent * tangent) * GELU_SCALE * (
        1.0 + 3.0 * CUBIC_COEFF * squared
    )
    return hidden, (back_grad * gelu_slope).astype(BF16)


def slot_of(offset):
    return 0 if offset == 0 else 2 * offset - 1 if offset > 0 else -2 * offset


def dot_nt(a, b):
    return lax.dot_general(a, b, (((1,), (1,)), ((), ())), preferred_element_type=F32)


def dot_tn(a, b):
    return lax.dot_general(a, b, (((0,), (0,)), ((), ())), preferred_element_type=F32)


def kernel(
    sizes,
    tokens_ref, w_up_ref, w_down_ref, cot_ref,
    grad_in_ref, grad_up_ref, grad_down_ref,
    near, far, rows, wide, up, down, up_t, down_t, part, other, act,
    pair_sum, pair_out, pair_in, back, x_out, x_in, back_out, back_in, own_sum, last_out, last_in, grad_up, grad_down,
    local_sem, near_send, near_recv, far_send, far_recv, y_send, y_recv, core_send, core_recv,
    z_send, z_recv, x_send, x_recv, back_send, back_recv, last_send, last_recv,
):
    n_gx, n_gy, n_gz = sizes
    n_hi = n_gz // 2
    own_rows = tokens_ref.shape[0]
    slot_rows = n_gx * own_rows
    total_rows = n_gy * slot_rows
    chunk_rows = total_rows // CHUNKS
    gx, gy, gz = lax.axis_index("gx"), lax.axis_index("gy"), lax.axis_index("gz")
    hi, core = gz // 2, gz % 2
    n_low = n_gx // N_X
    at_x, low = gx // n_low, gx % n_low

    def at_gx(j):
        return ((at_x + j // n_low) % N_X * n_low + (low + j % n_low) % n_low, gy, gz)

    def at_gy(j):
        return (gx, (gy + n_gy + j) % n_gy, gz)

    def at_hi(j):
        return (gx, gy, ((hi + n_hi + j) % n_hi) * 2 + core)

    other_core = (gx, gy, hi * 2 + 1 - core)

    load_up = pltpu.make_async_copy(w_up_ref, up, local_sem.at[0])
    load_down = pltpu.make_async_copy(w_down_ref, down, local_sem.at[1])
    load_tokens = pltpu.make_async_copy(tokens_ref, near.at[0, 0], local_sem.at[2])
    load_cot = pltpu.make_async_copy(cot_ref, near.at[0, 1], local_sem.at[3])
    load_tokens.start()
    load_cot.start()
    load_up.start()
    load_down.start()

    partners = [at_gx(j) for j in range(1, n_gx)] + [at_gy(j) for j in range(1, n_gy)]
    partners += [at_hi(1), at_hi(-1), other_core]
    barrier = pltpu.get_barrier_semaphore()
    for partner in partners:
        pl.semaphore_signal(barrier, inc=1, device_id=partner, device_id_type=MESH)
    load_tokens.wait()
    load_cot.wait()
    pl.semaphore_wait(barrier, len(partners))

    sent = []

    def send(src, dst, send_sem, recv_sem, device):
        copy = pltpu.make_async_remote_copy(
            src_ref=src, dst_ref=dst, send_sem=send_sem, recv_sem=recv_sem, device_id=device, device_id_type=MESH
        )
        copy.start()
        sent.append(copy)

    def arrived(dst, recv_sem):
        pltpu.make_async_remote_copy(
            src_ref=dst, dst_ref=dst, send_sem=recv_sem, recv_sem=recv_sem, device_id=other_core, device_id_type=MESH
        ).wait_recv()

    for j in range(1, n_gx):
        send(near.at[0], near.at[j], near_send.at[j], near_recv.at[j], at_gx(j))
    for n, offset in enumerate(FAR):
        send(near.at[0], far.at[n, 0], far_send.at[n], far_recv.at[n], at_gy(-offset))
    load_up.wait()
    load_down.wait()
    down_t[...] = down[...].T
    up_t[...] = up[...].T
    for j in range(n_gx):
        if j:
            arrived(near.at[j], near_recv.at[j])
        for which in range(2):
            wide[which, j * own_rows : (j + 1) * own_rows] = near[j, which].astype(F32)
    rows[:, :slot_rows] = wide[...].astype(BF16)

    n_far = len(FAR)

    def far_low():
        for n in range(n_far):
            arrived(far.at[n, 0], far_recv.at[n])
        for j in range(1, n_low):
            send(far.at[:, 0], far.at[:, j], far_send.at[n_far + j], far_recv.at[n_far + j], at_gx(j))

    def far_x():
        for j in range(1, n_low):
            arrived(far.at[:, j], far_recv.at[n_far + j])
        for j in range(1, N_X):
            at = n_far + n_low + j
            send(
                far.at[:, pl.ds(0, n_low)], far.at[:, pl.ds(j * n_low, n_low)],
                far_send.at[at], far_recv.at[at], at_gx(j * n_low),
            )

    def far_rows():
        for j in range(1, N_X):
            arrived(far.at[:, pl.ds(j * n_low, n_low)], far_recv.at[n_far + n_low + j])
        for n, offset in enumerate(FAR):
            for k in range(n_gx):
                for which in range(2):
                    wide[which, k * own_rows : (k + 1) * own_rows] = far[n, k, which].astype(F32)
            first = slot_of(offset) * slot_rows
            rows[:, first : first + slot_rows] = wide[...].astype(BF16)

    half = n_gy // 2
    piece = slot_rows // PIECES

    def hop(step, which, at, way):
        offsets = (step - 1, step) if way == 0 else (1 - step, -step)
        src, dst = (slot_of(o) * slot_rows + at * piece for o in offsets)
        return rows.at[which, src : src + piece], rows.at[which, dst : dst + piece]

    def ring(step, which, at, way):
        src, dst = hop(step, which, at, way)
        sems = (way, which, at, step)
        send(src, dst, y_send.at[sems], y_recv.at[sems], at_gy(-1 if way == 0 else 1))

    order = [(which, at, way) for at in range(PIECES) for which in range(2) for way in range(2)]

    def pass_on(step):
        for which, at, way in order:
            if step:
                arrived(hop(step, which, at, way)[1], y_recv.at[way, which, at, step])
            if step < STEPS:
                ring(step + 1, which, at, way)

    def chunk(c):
        return pl.ds(c * chunk_rows, chunk_rows)

    def forward(c):
        for which, value in enumerate(
            (
                jnp.dot(rows[0, chunk(c)], up[...], preferred_element_type=F32),
                jnp.dot(rows[1, chunk(c)], down_t[...], preferred_element_type=F32),
            )
        ):
            part[c, :, which] = value.reshape(n_gz, chunk_rows // n_gz, value.shape[1])
        theirs = part.at[c, pl.ds((1 - core) * n_hi, n_hi)]
        send(theirs, other.at[c], core_send.at[c, 0], core_recv.at[c, 0], other_core)

    towards = 1 - 2 * (hi % 2)
    partner = (at_hi(towards), at_hi(-towards))
    kept = ((hi // 2 + hi % 2) % 2, 2 + hi // 2)
    given = (1 - kept[0], 5 - kept[1])

    def chip_sum(c, tile):
        return part[c, core * n_hi + tile] + other[c, tile]

    def pair_send(c, step, which, to):
        at = (c, step, which)
        send(pair_out.at[at], pair_in.at[at], z_send.at[at], z_recv.at[at], partner[to])

    def pair_add(c, step, which):
        at = (c, step, which)
        arrived(pair_in.at[at], z_recv.at[at])
        pair_sum[c, which] += pair_in[at].astype(F32)

    def tile_of(c, tile, of=core):
        return act.at[c, of * n_hi + tile]

    def to_core(c, tile, at):
        send(tile_of(c, tile), tile_of(c, tile), core_send.at[c, at], core_recv.at[c, at], other_core)

    def e1(c):
        arrived(other.at[c], core_recv.at[c, 0])
        for which in range(2):
            pair_out[c, 0, which] = chip_sum(c, given[which]).astype(BF16)
            pair_send(c, 0, which, which)
        for which in range(2):
            pair_sum[c, which] = chip_sum(c, kept[which])

    def e2(c):
        for which in range(2):
            pair_add(c, 0, which)
            pair_out[c, 1, which] = pair_sum[c, which].astype(BF16)
            pair_send(c, 1, which, 1 - which)

    def e3(c):
        for which in range(2):
            pair_add(c, 1, which)
            hidden, pre_grad = activate(pair_sum[c, which, 0], pair_sum[c, which, 1])
            act[c, core * n_hi + kept[which], 0] = hidden
            act[c, core * n_hi + kept[which], 1] = pre_grad
            tile = tile_of(c, kept[which])
            send(tile, tile, z_send.at[c, 2, which], z_recv.at[c, 2, which], partner[which])
            to_core(c, kept[which], 1 + which)

    def e4(c):
        for which in range(2):
            arrived(tile_of(c, given[which]), z_recv.at[c, 2, which])
            to_core(c, given[which], 3 + which)

    def e6(c):
        for which in range(2):
            arrived(tile_of(c, kept[which], 1 - core), core_recv.at[c, 1 + which])
            arrived(tile_of(c, given[which], 1 - core), core_recv.at[c, 3 + which])

    def whole(c, which):
        return act[c, :, which].reshape(chunk_rows, act.shape[-1])

    x_rows = slot_rows // N_X
    slots = {slot_of(offset): offset for offset in range(1 - half, half + 1)}

    def finished(c):
        return [at for at in slots if c * chunk_rows < (at + 1) * slot_rows <= (c + 1) * chunk_rows]

    def group(at, j):
        start = at * slot_rows + j * x_rows
        return back[start : start + x_rows]

    def backward(c):
        first = c * chunk_rows
        back[first : first + chunk_rows] = jnp.dot(whole(c, 1), up_t[...], preferred_element_type=F32)
        done = sorted(finished(c))
        for j in range(1, N_X):
            for i, at in enumerate(done):
                x_out[c, j, i] = group(at, j).astype(BF16)
            send(
                x_out.at[c, j, pl.ds(0, len(done))], x_in.at[c, j, pl.ds(0, len(done))],
                x_send.at[c, j], x_recv.at[c, j], at_gx((N_X - j) * n_low),
            )

    def sum_x(c):
        done = sorted(finished(c))
        for j in range(1, N_X):
            arrived(x_in.at[c, j, pl.ds(0, len(done))], x_recv.at[c, j])
        for i, at in enumerate(done):
            total = group(at, 0)
            for j in range(1, N_X):
                total += x_in[c, j, i].astype(F32)
            if at == 0:
                own_sum[...] = total
            else:
                back_out[at] = total.astype(BF16)
                send(back_out.at[at], back_in.at[at], back_send.at[at], back_recv.at[at], at_gy(slots[at]))

    stores = (
        pltpu.make_async_copy(grad_up, grad_up_ref, local_sem.at[0]),
        pltpu.make_async_copy(grad_down, grad_down_ref, local_sem.at[1]),
    )

    def weights():
        hidden = jnp.concatenate([whole(c, 0) for c in range(CHUNKS)])
        pre_grad = jnp.concatenate([whole(c, 1) for c in range(CHUNKS)])
        grad_up[...] = dot_tn(rows[0], pre_grad).astype(BF16)
        stores[0].start()
        grad_down[...] = dot_tn(hidden, rows[1]).astype(BF16)
        stores[1].start()

    pass_on(0)
    far_low()
    pass_on(1)
    far_x()
    forward(0)
    pass_on(2)
    e1(0)
    far_rows()
    forward(1)
    e1(1)
    forward(2)
    e2(0)
    e1(2)
    e2(1)
    e3(0)
    e2(2)
    e3(1)
    e4(0)
    e3(2)
    e6(0)
    backward(0)
    e4(1)
    e6(1)
    backward(1)
    sum_x(0)
    e4(2)
    e6(2)
    backward(2)
    sum_x(1)
    weights()
    sum_x(2)

    for at in range(1, n_gy):
        arrived(back_in.at[at], back_recv.at[at])
        own_sum[...] += back_in[at].astype(F32)
    for j in range(1, n_low):
        last_out[j] = own_sum[j * own_rows : (j + 1) * own_rows].astype(BF16)
        send(last_out.at[j], last_in.at[j], last_send.at[j], last_recv.at[j], at_gx(n_low - j))
    result = own_sum[:own_rows]
    for j in range(1, n_low):
        arrived(last_in.at[j], last_recv.at[j])
        result += last_in[j].astype(F32)
    grad_in_ref[...] = result
    for store in stores:
        store.wait()
    for copy in sent:
        copy.wait_send()


def hand_over(*refs):
    buffers, (loaded, stored) = refs[6:9], refs[9:]
    loads, stores = [], []
    for src, held, dst in zip(refs[:3], buffers, refs[3:6]):
        parts = 4 if src.shape[0] % 64 == 0 else 1
        size = src.shape[0] // parts
        for p in range(parts):
            part, n = pl.ds(p * size, size), len(loads)
            loads.append(pltpu.make_async_copy(src.at[part], held.at[part], loaded.at[n]))
            stores.append(pltpu.make_async_copy(held.at[part], dst.at[part], stored.at[n]))
    for load in loads:
        load.start()
    for load, store in zip(loads, stores):
        load.wait()
        store.start()
    for store in stores:
        store.wait()


def on_device(sizes, tokens, w_up, w_down, cotangent):
    n_gx, n_gy, n_gz = sizes
    own_rows, width = tokens.shape
    units = w_up.shape[1]
    slot_rows = n_gx * own_rows
    total = slot_rows * n_gy
    n_hi = n_gz // 2
    r = total // CHUNKS // n_gz
    n_low, x_rows = n_gx // N_X, slot_rows // N_X
    dma = pltpu.SemaphoreType.DMA
    results = pl.pallas_call(
        functools.partial(kernel, sizes),
        out_shape=(
            jax.ShapeDtypeStruct((own_rows, width), F32),
            jax.ShapeDtypeStruct((width, units), BF16),
            jax.ShapeDtypeStruct((units, width), BF16),
        ),
        in_specs=[pl.BlockSpec(memory_space=pltpu.HBM)] * 4,
        out_specs=(
            pl.BlockSpec(memory_space=pltpu.VMEM),
            pl.BlockSpec(memory_space=pl.ANY),
            pl.BlockSpec(memory_space=pl.ANY),
        ),
        scratch_shapes=[
            pltpu.VMEM((n_gx, 2, own_rows, width), BF16),
            pltpu.VMEM((len(FAR), n_gx, 2, own_rows, width), BF16),
            pltpu.VMEM((2, total, width), BF16),
            pltpu.VMEM((2, slot_rows, width), F32),
            pltpu.VMEM((width, units), BF16),
            pltpu.VMEM((units, width), BF16),
            pltpu.VMEM((units, width), BF16),
            pltpu.VMEM((width, units), BF16),
            pltpu.VMEM((CHUNKS, n_gz, 2, r, units), F32),
            pltpu.VMEM((CHUNKS, n_hi, 2, r, units), F32),
            pltpu.VMEM((CHUNKS, n_gz, 2, r, units), BF16),
            pltpu.VMEM((CHUNKS, 2, 2, r, units), F32),
            pltpu.VMEM((CHUNKS, 2, 2, 2, r, units), BF16),
            pltpu.VMEM((CHUNKS, 2, 2, 2, r, units), BF16),
            pltpu.VMEM((total, width), F32),
            pltpu.VMEM((CHUNKS, N_X, n_gy // 2, x_rows, width), BF16),
            pltpu.VMEM((CHUNKS, N_X, n_gy // 2, x_rows, width), BF16),
            pltpu.VMEM((n_gy, x_rows, width), BF16),
            pltpu.VMEM((n_gy, x_rows, width), BF16),
            pltpu.VMEM((x_rows, width), F32),
            pltpu.VMEM((n_low, own_rows, width), BF16),
            pltpu.VMEM((n_low, own_rows, width), BF16),
            pltpu.VMEM((width, units), BF16),
            pltpu.VMEM((units, width), BF16),
            dma((4,)),
            dma((n_gx,)),
            dma((n_gx,)),
            dma((len(FAR) + n_low + N_X,)),
            dma((len(FAR) + n_low + N_X,)),
            dma((2, 2, PIECES, n_gy // 2 + 1)),
            dma((2, 2, PIECES, n_gy // 2 + 1)),
            dma((CHUNKS, 5)),
            dma((CHUNKS, 5)),
            dma((CHUNKS, 3, 2)),
            dma((CHUNKS, 3, 2)),
            dma((CHUNKS, N_X)),
            dma((CHUNKS, N_X)),
            dma((n_gy,)),
            dma((n_gy,)),
            dma((n_gx // N_X,)),
            dma((n_gx // N_X,)),
        ],
        compiler_params=pltpu.CompilerParams(
            collective_id=0, has_side_effects=True, vmem_limit_bytes=VMEM_LIMIT
        ),
    )(tokens, w_up, w_down, cotangent)
    return pl.pallas_call(
        hand_over,
        out_shape=tuple(jax.ShapeDtypeStruct(a.shape, a.dtype) for a in results),
        in_specs=[pl.BlockSpec(memory_space=pl.ANY)] * 3,
        out_specs=(pl.BlockSpec(memory_space=pl.ANY),) * 3,
        scratch_shapes=[pltpu.VMEM(a.shape, a.dtype) for a in results] + [dma((9,)), dma((9,))],
        compiler_params=pltpu.CompilerParams(vmem_limit_bytes=VMEM_LIMIT),
    )(*results)


def solution(mesh):
    sizes = tuple(mesh.shape[axis] for axis in ("gx", "gy", "gz"))
    placed = (
        P(("gx", "gy"), "gz"),
        P("gz", ("gx", "gy")),
        P(("gx", "gy"), "gz"),
        P(("gx", "gy"), "gz"),
    )
    return jax.shard_map(
        functools.partial(on_device, sizes),
        mesh=mesh,
        in_specs=placed,
        out_specs=(P(("gx", "gy"), "gz"), P("gz", ("gx", "gy")), P(("gx", "gy"), "gz")),
        check_vma=False,
    )
```

```python
import functools
import math

import jax
import jax.numpy as jnp
from jax import lax
from jax.experimental import pallas as pl
from jax.experimental.pallas import tpu as pltpu
from jax.sharding import PartitionSpec as P

GELU_SCALE = math.sqrt(2.0 / math.pi)
CUBIC_COEFF = 0.044715
MESH = pl.DeviceIdType.MESH
BF16, F32 = jnp.bfloat16, jnp.float32
CHUNKS = 3
PIECES = 3
FAR = (3, -3, 4)
STEPS = 2
VMEM_LIMIT = 63 * 1024 * 1024
N_X = 4


def activate(pre_act, back_grad):
    squared = pre_act * pre_act
    tangent = jnp.tanh(GELU_SCALE * pre_act * (1.0 + CUBIC_COEFF * squared))
    hidden = (0.5 * pre_act * (1.0 + tangent)).astype(BF16)
    gelu_slope = 0.5 * (1.0 + tangent) + 0.5 * pre_act * (1.0 - tangent * tangent) * GELU_SCALE * (
        1.0 + 3.0 * CUBIC_COEFF * squared
    )
    return hidden, (back_grad * gelu_slope).astype(BF16)


def slot_of(offset):
    return 0 if offset == 0 else 2 * offset - 1 if offset > 0 else -2 * offset


def dot_nt(a, b):
    return lax.dot_general(a, b, (((1,), (1,)), ((), ())), preferred_element_type=F32)


def dot_tn(a, b):
    return lax.dot_general(a, b, (((0,), (0,)), ((), ())), preferred_element_type=F32)


def kernel(
    sizes,
    tokens_ref, w_up_ref, w_down_ref, cot_ref,
    grad_in_ref, grad_up_ref, grad_down_ref,
    near, far, rows, wide, up, down, up_t, down_t, part, other, act,
    pair_sum, pair_out, pair_in, back, x_out, x_in, own_sum, last_out, last_in, grad_up, grad_down,
    local_sem, near_send, near_recv, far_send, far_recv, y_send, y_recv, core_send, core_recv,
    z_send, z_recv, x_send, x_recv, last_send, last_recv,
):
    n_gx, n_gy, n_gz = sizes
    n_hi = n_gz // 2
    own_rows = tokens_ref.shape[0]
    slot_rows = n_gx * own_rows
    total_rows = n_gy * slot_rows
    chunk_rows = total_rows // CHUNKS
    gx, gy, gz = lax.axis_index("gx"), lax.axis_index("gy"), lax.axis_index("gz")
    hi, core = gz // 2, gz % 2
    n_low = n_gx // N_X
    at_x, low = gx // n_low, gx % n_low

    def at_gx(j):
        return ((at_x + j // n_low) % N_X * n_low + (low + j % n_low) % n_low, gy, gz)

    def at_gy(j):
        return (gx, (gy + n_gy + j) % n_gy, gz)

    def at_hi(j):
        return (gx, gy, ((hi + n_hi + j) % n_hi) * 2 + core)

    other_core = (gx, gy, hi * 2 + 1 - core)

    load_up = pltpu.make_async_copy(w_up_ref, up, local_sem.at[0])
    load_down = pltpu.make_async_copy(w_down_ref, down, local_sem.at[1])
    load_tokens = pltpu.make_async_copy(tokens_ref, near.at[0, 0], local_sem.at[2])
    load_cot = pltpu.make_async_copy(cot_ref, near.at[0, 1], local_sem.at[3])
    load_tokens.start()
    load_cot.start()
    load_up.start()
    load_down.start()

    partners = [at_gx(j) for j in range(1, n_gx)] + [at_gy(j) for j in range(1, n_gy)]
    partners += [at_hi(1), at_hi(-1), other_core]
    barrier = pltpu.get_barrier_semaphore()
    for partner in partners:
        pl.semaphore_signal(barrier, inc=1, device_id=partner, device_id_type=MESH)
    load_tokens.wait()
    load_cot.wait()
    pl.semaphore_wait(barrier, len(partners))

    sent = []

    def send(src, dst, send_sem, recv_sem, device):
        copy = pltpu.make_async_remote_copy(
            src_ref=src, dst_ref=dst, send_sem=send_sem, recv_sem=recv_sem, device_id=device, device_id_type=MESH
        )
        copy.start()
        sent.append(copy)

    def arrived(dst, recv_sem):
        pltpu.make_async_remote_copy(
            src_ref=dst, dst_ref=dst, send_sem=recv_sem, recv_sem=recv_sem, device_id=other_core, device_id_type=MESH
        ).wait_recv()

    for j in range(1, n_gx):
        send(near.at[0], near.at[j], near_send.at[j], near_recv.at[j], at_gx(j))
    for n, offset in enumerate(FAR):
        send(near.at[0], far.at[n, 0], far_send.at[n], far_recv.at[n], at_gy(-offset))
    load_up.wait()
    load_down.wait()
    down_t[...] = down[...].T
    up_t[...] = up[...].T
    for j in range(n_gx):
        if j:
            arrived(near.at[j], near_recv.at[j])
        for which in range(2):
            wide[which, j * own_rows : (j + 1) * own_rows] = near[j, which].astype(F32)
    rows[:, :slot_rows] = wide[...].astype(BF16)

    n_far = len(FAR)

    def far_low():
        for n in range(n_far):
            arrived(far.at[n, 0], far_recv.at[n])
        for j in range(1, n_low):
            send(far.at[:, 0], far.at[:, j], far_send.at[n_far + j], far_recv.at[n_far + j], at_gx(j))

    def far_x():
        for j in range(1, n_low):
            arrived(far.at[:, j], far_recv.at[n_far + j])
        for j in range(1, N_X):
            at = n_far + n_low + j
            send(
                far.at[:, pl.ds(0, n_low)], far.at[:, pl.ds(j * n_low, n_low)],
                far_send.at[at], far_recv.at[at], at_gx(j * n_low),
            )

    def far_rows():
        for j in range(1, N_X):
            arrived(far.at[:, pl.ds(j * n_low, n_low)], far_recv.at[n_far + n_low + j])
        for n, offset in enumerate(FAR):
            for k in range(n_gx):
                for which in range(2):
                    wide[which, k * own_rows : (k + 1) * own_rows] = far[n, k, which].astype(F32)
            first = slot_of(offset) * slot_rows
            rows[:, first : first + slot_rows] = wide[...].astype(BF16)

    half = n_gy // 2
    piece = slot_rows // PIECES

    def hop(step, which, at, way):
        offsets = (step - 1, step) if way == 0 else (1 - step, -step)
        src, dst = (slot_of(o) * slot_rows + at * piece for o in offsets)
        return rows.at[which, src : src + piece], rows.at[which, dst : dst + piece]

    def ring(step, which, at, way):
        src, dst = hop(step, which, at, way)
        sems = (way, which, at, step)
        send(src, dst, y_send.at[sems], y_recv.at[sems], at_gy(-1 if way == 0 else 1))

    order = [(which, at, way) for at in range(PIECES) for which in range(2) for way in range(2)]

    def pass_on(step):
        for which, at, way in order:
            if step:
                arrived(hop(step, which, at, way)[1], y_recv.at[way, which, at, step])
            if step < STEPS:
                ring(step + 1, which, at, way)

    def chunk(c):
        return pl.ds(c * chunk_rows, chunk_rows)

    def forward(c):
        for which, value in enumerate(
            (
                jnp.dot(rows[0, chunk(c)], up[...], preferred_element_type=F32),
                jnp.dot(rows[1, chunk(c)], down_t[...], preferred_element_type=F32),
            )
        ):
            part[c, :, which] = value.reshape(n_gz, chunk_rows // n_gz, value.shape[1])
        theirs = part.at[c, pl.ds((1 - core) * n_hi, n_hi)]
        send(theirs, other.at[c], core_send.at[c, 0], core_recv.at[c, 0], other_core)

    towards = 1 - 2 * (hi % 2)
    partner = (at_hi(towards), at_hi(-towards))
    kept = ((hi // 2 + hi % 2) % 2, 2 + hi // 2)
    given = (1 - kept[0], 5 - kept[1])

    def chip_sum(c, tile):
        return part[c, core * n_hi + tile] + other[c, tile]

    def pair_send(c, step, which, to):
        at = (c, step, which)
        send(pair_out.at[at], pair_in.at[at], z_send.at[at], z_recv.at[at], partner[to])

    def pair_add(c, step, which):
        at = (c, step, which)
        arrived(pair_in.at[at], z_recv.at[at])
        pair_sum[c, which] += pair_in[at].astype(F32)

    def tile_of(c, tile, of=core):
        return act.at[c, of * n_hi + tile]

    def to_core(c, tile, at):
        send(tile_of(c, tile), tile_of(c, tile), core_send.at[c, at], core_recv.at[c, at], other_core)

    def e1(c):
        arrived(other.at[c], core_recv.at[c, 0])
        for which in range(2):
            pair_out[c, 0, which] = chip_sum(c, given[which]).astype(BF16)
            pair_send(c, 0, which, which)
        for which in range(2):
            pair_sum[c, which] = chip_sum(c, kept[which])

    def e2(c):
        for which in range(2):
            pair_add(c, 0, which)
            pair_out[c, 1, which] = pair_sum[c, which].astype(BF16)
            pair_send(c, 1, which, 1 - which)

    def e3(c):
        for which in range(2):
            pair_add(c, 1, which)
            hidden, pre_grad = activate(pair_sum[c, which, 0], pair_sum[c, which, 1])
            act[c, core * n_hi + kept[which], 0] = hidden
            act[c, core * n_hi + kept[which], 1] = pre_grad
            tile = tile_of(c, kept[which])
            send(tile, tile, z_send.at[c, 2, which], z_recv.at[c, 2, which], partner[which])
            to_core(c, kept[which], 1 + which)

    def e4(c):
        for which in range(2):
            arrived(tile_of(c, given[which]), z_recv.at[c, 2, which])
            to_core(c, given[which], 3 + which)

    def e6(c):
        for which in range(2):
            arrived(tile_of(c, kept[which], 1 - core), core_recv.at[c, 1 + which])
            arrived(tile_of(c, given[which], 1 - core), core_recv.at[c, 3 + which])

    def whole(c, which):
        return act[c, :, which].reshape(chunk_rows, act.shape[-1])

    x_rows = slot_rows // N_X
    slots = {slot_of(offset): offset for offset in range(1 - half, half + 1)}

    def finished(c):
        return [at for at in slots if c * chunk_rows < (at + 1) * slot_rows <= (c + 1) * chunk_rows]

    def group(at, j):
        start = at * slot_rows + j * x_rows
        return back[start : start + x_rows]

    def backward(c):
        first = c * chunk_rows
        back[first : first + chunk_rows] = jnp.dot(whole(c, 1), up_t[...], preferred_element_type=F32)
        done = sorted(finished(c))
        for j in range(1, N_X):
            for i, at in enumerate(done):
                x_out[c, j, i] = group(at, j).astype(BF16)
            send(
                x_out.at[c, j, pl.ds(0, len(done))], x_in.at[c, j, pl.ds(0, len(done))],
                x_send.at[c, j], x_recv.at[c, j], at_gx((N_X - j) * n_low),
            )

    def sum_x(c):
        done = sorted(finished(c))
        for j in range(1, N_X):
            arrived(x_in.at[c, j, pl.ds(0, len(done))], x_recv.at[c, j])
        for i, at in enumerate(done):
            total = group(at, 0)
            for j in range(1, N_X):
                total += x_in[c, j, i].astype(F32)
            for k in range(n_low):
                value = total[k * own_rows : (k + 1) * own_rows]
                if at == 0 and k == 0:
                    own_sum[...] = value
                else:
                    last_out[at, k] = value.astype(BF16)
                    owner = at_x * n_low + (low + n_low - k) % n_low, (gy + n_gy + slots[at]) % n_gy, gz
                    send(last_out.at[at, k], last_in.at[at, k], last_send.at[at, k], last_recv.at[at, k], owner)

    stores = (
        pltpu.make_async_copy(grad_up, grad_up_ref, local_sem.at[0]),
        pltpu.make_async_copy(grad_down, grad_down_ref, local_sem.at[1]),
    )

    def weights():
        hidden = jnp.concatenate([whole(c, 0) for c in range(CHUNKS)])
        pre_grad = jnp.concatenate([whole(c, 1) for c in range(CHUNKS)])
        grad_up[...] = dot_tn(rows[0], pre_grad).astype(BF16)
        stores[0].start()
        grad_down[...] = dot_tn(hidden, rows[1]).astype(BF16)
        stores[1].start()

    pass_on(0)
    far_low()
    pass_on(1)
    far_x()
    forward(0)
    pass_on(2)
    e1(0)
    far_rows()
    forward(1)
    e1(1)
    forward(2)
    e2(0)
    e1(2)
    e2(1)
    e3(0)
    e2(2)
    e3(1)
    e4(0)
    e3(2)
    e6(0)
    backward(0)
    e4(1)
    e6(1)
    backward(1)
    sum_x(0)
    e4(2)
    e6(2)
    backward(2)
    sum_x(1)
    weights()
    sum_x(2)

    result = own_sum[...]
    for at in range(n_gy):
        for k in range(n_low):
            if at or k:
                arrived(last_in.at[at, k], last_recv.at[at, k])
                result += last_in[at, k].astype(F32)
    grad_in_ref[...] = result
    for store in stores:
        store.wait()
    for copy in sent:
        copy.wait_send()


def hand_over(*refs):
    buffers, (loaded, stored) = refs[6:9], refs[9:]
    loads, stores = [], []
    for src, held, dst in zip(refs[:3], buffers, refs[3:6]):
        parts = 4 if src.shape[0] % 64 == 0 else 1
        size = src.shape[0] // parts
        for p in range(parts):
            part, n = pl.ds(p * size, size), len(loads)
            loads.append(pltpu.make_async_copy(src.at[part], held.at[part], loaded.at[n]))
            stores.append(pltpu.make_async_copy(held.at[part], dst.at[part], stored.at[n]))
    for load in loads:
        load.start()
    for load, store in zip(loads, stores):
        load.wait()
        store.start()
    for store in stores:
        store.wait()


def on_device(sizes, tokens, w_up, w_down, cotangent):
    n_gx, n_gy, n_gz = sizes
    own_rows, width = tokens.shape
    units = w_up.shape[1]
    slot_rows = n_gx * own_rows
    total = slot_rows * n_gy
    n_hi = n_gz // 2
    r = total // CHUNKS // n_gz
    n_low, x_rows = n_gx // N_X, slot_rows // N_X
    dma = pltpu.SemaphoreType.DMA
    results = pl.pallas_call(
        functools.partial(kernel, sizes),
        out_shape=(
            jax.ShapeDtypeStruct((own_rows, width), F32),
            jax.ShapeDtypeStruct((width, units), BF16),
            jax.ShapeDtypeStruct((units, width), BF16),
        ),
        in_specs=[pl.BlockSpec(memory_space=pltpu.HBM)] * 4,
        out_specs=(
            pl.BlockSpec(memory_space=pltpu.VMEM),
            pl.BlockSpec(memory_space=pl.ANY),
            pl.BlockSpec(memory_space=pl.ANY),
        ),
        scratch_shapes=[
            pltpu.VMEM((n_gx, 2, own_rows, width), BF16),
            pltpu.VMEM((len(FAR), n_gx, 2, own_rows, width), BF16),
            pltpu.VMEM((2, total, width), BF16),
            pltpu.VMEM((2, slot_rows, width), F32),
            pltpu.VMEM((width, units), BF16),
            pltpu.VMEM((units, width), BF16),
            pltpu.VMEM((units, width), BF16),
            pltpu.VMEM((width, units), BF16),
            pltpu.VMEM((CHUNKS, n_gz, 2, r, units), F32),
            pltpu.VMEM((CHUNKS, n_hi, 2, r, units), F32),
            pltpu.VMEM((CHUNKS, n_gz, 2, r, units), BF16),
            pltpu.VMEM((CHUNKS, 2, 2, r, units), F32),
            pltpu.VMEM((CHUNKS, 2, 2, 2, r, units), BF16),
            pltpu.VMEM((CHUNKS, 2, 2, 2, r, units), BF16),
            pltpu.VMEM((total, width), F32),
            pltpu.VMEM((CHUNKS, N_X, n_gy // 2, x_rows, width), BF16),
            pltpu.VMEM((CHUNKS, N_X, n_gy // 2, x_rows, width), BF16),
            pltpu.VMEM((own_rows, width), F32),
            pltpu.VMEM((n_gy, n_low, own_rows, width), BF16),
            pltpu.VMEM((n_gy, n_low, own_rows, width), BF16),
            pltpu.VMEM((width, units), BF16),
            pltpu.VMEM((units, width), BF16),
            dma((4,)),
            dma((n_gx,)),
            dma((n_gx,)),
            dma((len(FAR) + n_low + N_X,)),
            dma((len(FAR) + n_low + N_X,)),
            dma((2, 2, PIECES, n_gy // 2 + 1)),
            dma((2, 2, PIECES, n_gy // 2 + 1)),
            dma((CHUNKS, 5)),
            dma((CHUNKS, 5)),
            dma((CHUNKS, 3, 2)),
            dma((CHUNKS, 3, 2)),
            dma((CHUNKS, N_X)),
            dma((CHUNKS, N_X)),
            dma((n_gy, n_gx // N_X)),
            dma((n_gy, n_gx // N_X)),
        ],
        compiler_params=pltpu.CompilerParams(
            collective_id=0, has_side_effects=True, vmem_limit_bytes=VMEM_LIMIT
        ),
    )(tokens, w_up, w_down, cotangent)
    return pl.pallas_call(
        hand_over,
        out_shape=tuple(jax.ShapeDtypeStruct(a.shape, a.dtype) for a in results),
        in_specs=[pl.BlockSpec(memory_space=pl.ANY)] * 3,
        out_specs=(pl.BlockSpec(memory_space=pl.ANY),) * 3,
        scratch_shapes=[pltpu.VMEM(a.shape, a.dtype) for a in results] + [dma((9,)), dma((9,))],
        compiler_params=pltpu.CompilerParams(vmem_limit_bytes=VMEM_LIMIT),
    )(*results)


def solution(mesh):
    sizes = tuple(mesh.shape[axis] for axis in ("gx", "gy", "gz"))
    placed = (
        P(("gx", "gy"), "gz"),
        P("gz", ("gx", "gy")),
        P(("gx", "gy"), "gz"),
        P(("gx", "gy"), "gz"),
    )
    return jax.shard_map(
        functools.partial(on_device, sizes),
        mesh=mesh,
        in_specs=placed,
        out_specs=(P(("gx", "gy"), "gz"), P("gz", ("gx", "gy")), P(("gx", "gy"), "gz")),
        check_vma=False,
    )
```
